32 devices in a mesh: seq: 16 (over z, y, x), vis: 2 (over core).
Axes of the slice: x: 2, y: 2, z: 4, core: 2. Of those that a mesh axis runs over, the one named last changes fastest.
Arguments:
- queries: bfloat16 [4096, 4096], P('seq', 'vis'), may hold values from -120 to 120
- keys: bfloat16 [64, 8, 512], P('seq', 'vis'), may hold values from -7 to 7
- values: bfloat16 [64, 8, 512], P('seq', 'vis'), may hold values from -6 to 6
- grad_out: bfloat16 [4096, 4096], P('seq', 'vis'), may hold values from -6 to 6
- block_map: int32 [16, 8], replicated, may hold values from 0 to 63, as said below
- block_count: int32 [16], replicated, may hold values from 6 to 8, as said below
Outputs:
- grad_queries: bfloat16 [4096, 4096], P('seq', 'vis')
- log_totals: float32 [32, 4096], P('vis', 'seq')
- grad_keys: bfloat16 [64, 8, 512], P('seq', 'vis')
- grad_values: bfloat16 [64, 8, 512], P('seq', 'vis')
The draws below stay inside these ranges and needn't reach their ends.
Inputs may be any that keep to these rules, and one draw needn't show every extreme that they name: `block_map`: block b belongs to seq index b // 4; the 8 blocks that one span names belong to 8 different seq indices. `block_count`: some span attends all 8 of its named blocks.
All inputs are finite; a program needn't handle non-finite values.
Results may differ from the reference program's by a relative error of at most 0.014.
Values may be sent and summed in bfloat16 or wider, within the bound.
No kernel may reach another device: no remote copies, remote signals or barrier semaphores. Data moves between devices by JAX's collectives and lax.ppermute only.
A program may use at most 64 MiB of HBM per device.

```python
import math
import jax
import jax.numpy as jnp
from jax import lax

HEADS = 32
KV_HEADS = 4
HEAD_DIM = 128
BLK = 8
TOK_DEV = 256
BPD = 4
GROUP = 8
HCOL = 4096
KVCOL = 512
NB = 8
NBLK = 64
TEXT = 4096
N_SEQ = 16


def block_table(key):
    base_key = jax.random.fold_in(key, 101)
    span_keys = jax.random.split(base_key, N_SEQ)
    owners = jax.vmap(lambda span_key: jax.random.permutation(span_key, N_SEQ)[:NB])(span_keys)
    local_blocks = jax.random.randint(jax.random.fold_in(key, 102), (N_SEQ, NB), 0, BPD)
    return (owners * BPD + local_blocks).astype(jnp.int32)


def key_table(key):
    base_rows = jax.random.normal(jax.random.fold_in(key, 201), (NBLK, BLK, KVCOL), jnp.float32)
    return base_rows


def draw_block_map(key, part):
    return block_table(key)


def draw_block_count(key, part):
    counts = jax.random.randint(jax.random.fold_in(key, 103), (N_SEQ,), NB - NB // 4, NB + 1)
    fullest = jax.random.randint(jax.random.fold_in(key, 104), (), 0, N_SEQ)
    counts = jnp.where(jnp.arange(N_SEQ) == fullest, NB, counts)
    return counts.astype(jnp.int32)


def draw_keys(key, part):
    return key_table(key).astype(jnp.bfloat16)


def draw_queries(key, part):
    query_rows = jax.random.normal(jax.random.fold_in(key, 301), (TEXT, HCOL), jnp.float32)
    query_rows = jnp.clip(query_rows, -6.0, 6.0)
    return query_rows.astype(jnp.bfloat16)


def levels(key, dims, pieces, low, high):
    gain = 1.0
    for position, parts in pieces:
        heights = jax.random.uniform(jax.random.fold_in(jax.random.fold_in(key, 6), position), (parts,), jnp.float32, low / len(pieces), high / len(pieces))
        gain = gain * jnp.repeat(jnp.exp(heights), dims[position] // parts).reshape((-1,) + (1,) * (len(dims) - 1 - position))
    return gain


def centred(own_key, extent, scale, limit, pieces=(), kind=jnp.bfloat16):
    drawn = scale * jax.random.normal(own_key, extent, jnp.float32)
    if pieces:
        drawn = drawn * levels(own_key, extent, pieces, -0.22, 0.18)
    return jnp.clip(drawn, -limit, limit).astype(kind)


def setup_inputs(seed: int = 0) -> dict:
    key_of = jax.random.split(jax.random.key(seed), 7)
    return {
        "queries": draw_queries(jax.random.fold_in(key_of[6], 71), 0),
        "keys": draw_keys(jax.random.fold_in(key_of[6], 71), 0),
        "values": centred(key_of[2], (NBLK, BLK, KVCOL), 1.0, 6.0, ((0, 16), (1, 2))),
        "grad_out": centred(key_of[3], (TEXT, HCOL), 1.0, 6.0, ((0, 16), (1, 2))),
        "block_map": draw_block_map(jax.random.fold_in(key_of[6], 71), 0),
        "block_count": draw_block_count(jax.random.fold_in(key_of[6], 71), 0),
    }


def reference(queries, keys, values, grad_out, block_map, block_count):
    score_scale = 1.0 / math.sqrt(HEAD_DIM)
    keys_per = NB * BLK

    def span(totals_in, span_id):
        total_keys, total_values = totals_in
        row_start = span_id * TOK_DEV
        q_rows = lax.dynamic_slice_in_dim(queries, row_start, TOK_DEV, 0).astype(jnp.float32).reshape(TOK_DEV, KV_HEADS, GROUP, HEAD_DIM)
        g_rows = lax.dynamic_slice_in_dim(grad_out, row_start, TOK_DEV, 0).astype(jnp.float32).reshape(TOK_DEV, KV_HEADS, GROUP, HEAD_DIM)
        row_ids = block_map[span_id].astype(jnp.int32)
        key_rows = keys[row_ids].astype(jnp.float32).reshape(keys_per, KV_HEADS, HEAD_DIM)
        value_rows = values[row_ids].astype(jnp.float32).reshape(keys_per, KV_HEADS, HEAD_DIM)
        live_blocks = jnp.arange(NB, dtype=jnp.int32) < block_count[span_id]
        key_live = jnp.repeat(live_blocks, BLK)
        scores = jnp.einsum('tgrd,kgd->grtk', q_rows, key_rows) * score_scale
        scores = jnp.where(key_live[None, None, None, :], scores, -1e+30)
        row_max = lax.optimization_barrier(jnp.max(scores, axis=3))
        weights = jnp.exp(scores - row_max[..., None])
        totals = lax.optimization_barrier(jnp.sum(weights, axis=3))
        probs_full = weights / totals[..., None]
        probs_low = lax.optimization_barrier(probs_full.astype(jnp.bfloat16)).astype(jnp.float32)
        context = jnp.einsum('grtk,kgd->tgrd', probs_low, value_rows)
        delta_row = lax.optimization_barrier(jnp.sum(g_rows * context, axis=3))
        value_part = jnp.einsum('grtk,tgrd->kgd', probs_low, g_rows)
        grad_probs = jnp.einsum('tgrd,kgd->grtk', g_rows, value_rows)
        grad_scores = probs_full * (grad_probs - jnp.transpose(delta_row, (1, 2, 0))[..., None])
        grad_scores = lax.optimization_barrier(grad_scores.astype(jnp.bfloat16)).astype(jnp.float32)
        grad_query = jnp.einsum('grtk,kgd->tgrd', grad_scores, key_rows) * score_scale
        key_part = jnp.einsum('grtk,tgrd->kgd', grad_scores, q_rows) * score_scale
        total_keys = total_keys.at[row_ids].add(key_part.reshape(NB, BLK, KVCOL))
        total_values = total_values.at[row_ids].add(value_part.reshape(NB, BLK, KVCOL))
        log_rows = (row_max + jnp.log(totals)).reshape(HEADS, TOK_DEV)
        return ((total_keys, total_values), (grad_query.reshape(TOK_DEV, HCOL).astype(jnp.bfloat16), log_rows))
    zeros = jnp.zeros((NBLK, BLK, KVCOL), jnp.float32)
    (sum_keys, sum_values), (grad_rows, log_rows) = lax.scan(span, (zeros, zeros), jnp.arange(N_SEQ, dtype=jnp.int32))
    log_totals = jnp.transpose(log_rows, (1, 0, 2)).reshape(HEADS, TEXT)
    return (grad_rows.reshape(TEXT, HCOL), log_totals, sum_keys.astype(jnp.bfloat16), sum_values.astype(jnp.bfloat16))
```

```python
import functools
import math

import jax
import jax.numpy as jnp
from jax import lax
from jax.experimental import pallas as pl
from jax.experimental.pallas import tpu as pltpu
from jax.sharding import PartitionSpec as P

HEAD_DIM = 128
GROUP = 8
BF16 = jnp.bfloat16
F32 = jnp.float32
VMEM = pl.BlockSpec(memory_space=pltpu.VMEM)


def iota(shape, dim):
    return lax.broadcasted_iota(jnp.int32, shape, dim)


def dot(left, right, left_dim=1, right_dim=0):
    return lax.dot_general(
        left, right, (((left_dim,), (right_dim,)), ((), ())), preferred_element_type=F32
    )


def slot_of_span(block_map, block_count, me, per_owner):
    live = iota(block_map.shape, 1) < block_count
    asked = live & (block_map // per_owner == me)
    return jnp.sum(jnp.where(asked, block_map % per_owner + 1, 0), axis=1, keepdims=True) - 1


def route(slot, rows, per_owner, span_dim):
    spans = slot.shape[0]
    span_rows, slot_rows = spans * 2 * rows, 2 * per_owner * rows
    expand = (iota((span_rows, spans), 0) // (2 * rows) == iota((span_rows, spans), 1)).astype(BF16)
    if span_dim == 0:
        shape = (span_rows, slot_rows)
        want = dot(expand, jnp.broadcast_to(slot, (spans, slot_rows)).astype(BF16))
    else:
        shape = (slot_rows, span_rows)
        want = dot(jnp.broadcast_to(slot, (spans, slot_rows)).astype(BF16), expand, 0, 1)
    place = iota(shape, span_dim) % (2 * rows)
    have = iota(shape, 1 - span_dim)
    have_slot = have % (per_owner * rows) // rows
    have_place = have // (per_owner * rows) * rows + have % rows
    return ((want == have_slot.astype(F32)) & (place == have_place)).astype(BF16)


def send_kernel(width, starts, rows, per_owner, me_ref, map_ref, count_ref, keys_ref, values_ref, out_ref):
    slot = jnp.maximum(slot_of_span(map_ref[...], count_ref[...], me_ref[0], per_owner), 0)
    pick = route(slot, rows, per_owner, 0)
    stacked = jnp.concatenate([keys_ref[...], values_ref[...]], axis=0)
    for core, start in enumerate(starts):
        out_ref[core] = dot(pick, stacked[:, start : start + width]).astype(BF16)


def sum_kernel(width, starts, rows, per_owner, me_ref, map_ref, count_ref, terms_ref, keys_ref, values_ref):
    slot = slot_of_span(map_ref[...], count_ref[...], me_ref[0], per_owner)
    pick = route(slot, rows, per_owner, 1)
    half = per_owner * rows
    done = {}
    for core, start in enumerate(starts):
        part = dot(pick, terms_ref[core])
        done[start] = done[start] + part if start in done else part
    for start, total in done.items():
        keys_ref[:, start : start + width] = total[:half].astype(BF16)
        values_ref[:, start : start + width] = total[half:].astype(BF16)


def attend_kernel(
    rows, per_owner, cores, spans, me_ref, map_ref, count_ref, q_ref, g_ref, rows_ref, gq_ref, log_ref, terms_ref
):
    score_scale = 1.0 / math.sqrt(HEAD_DIM)
    me = me_ref[0]
    most = map_ref.shape[1]
    block_rows = cores * rows
    keys = most * block_rows
    kv_heads = rows_ref.shape[1] // HEAD_DIM
    heads = q_ref.shape[1] // HEAD_DIM
    tokens = q_ref.shape[0]
    per_kv = heads // kv_heads
    row = map_ref[pl.ds(me, 1), :]
    count = count_ref[pl.ds(me, 1), :]

    shape = (2 * keys, rows_ref.shape[0])
    mine, theirs = iota((2 * keys, 1), 0), iota(shape, 1)
    block = mine % keys // block_rows
    owner = jnp.sum(jnp.where(iota((2 * keys, most), 1) == block, row // per_owner, 0), axis=1, keepdims=True)
    place = ((mine % block_rows // rows * spans + owner) * 2 + mine // keys) * rows + mine % rows
    place = jnp.where(block < count, place, -1)
    pick = (place == theirs).astype(BF16)
    fetched = dot(pick, rows_ref[...]).astype(BF16)
    live = (iota((2, keys, tokens), 1) // block_rows) < count.reshape(1, 1, 1)

    gk_parts, gv_parts = [], []
    for kv in range(kv_heads):
        cols = slice(kv * HEAD_DIM, (kv + 1) * HEAD_DIM)
        k, v = fetched[:keys, cols], fetched[keys:, cols]
        zero = jnp.zeros_like(k)
        k2 = jnp.concatenate([jnp.concatenate([k, zero], 1), jnp.concatenate([zero, k], 1)], 0)
        v2 = jnp.concatenate([jnp.concatenate([v, zero], 1), jnp.concatenate([zero, v], 1)], 0)
        gk = jnp.zeros((2 * keys, 2 * HEAD_DIM), F32)
        gv = jnp.zeros((2 * keys, 2 * HEAD_DIM), F32)
        for pair in range(per_kv // 2):
            head = kv * per_kv + 2 * pair
            at = slice(head * HEAD_DIM, (head + 2) * HEAD_DIM)
            q, g = q_ref[:, at], g_ref[:, at]
            scores = (dot(k2, q, 1, 1) * score_scale).reshape(2, keys, tokens)
            scores = jnp.where(live, scores, -1e30)
            row_max = jnp.max(scores, axis=1, keepdims=True)
            weights = jnp.exp(scores - row_max)
            totals = jnp.sum(weights, axis=1, keepdims=True)
            probs = weights * (1.0 / totals)
            log_ref[head : head + 2, :] = (row_max + jnp.log(totals)).reshape(2, tokens)
            low = probs.astype(BF16)
            grad_probs = dot(v2, g, 1, 1).reshape(2, keys, tokens)
            delta = jnp.sum(low.astype(F32) * grad_probs, axis=1, keepdims=True)
            gs = (probs * (grad_probs - delta)).astype(BF16).reshape(2 * keys, tokens)
            gv += dot(low.reshape(2 * keys, tokens), g)
            gk += dot(gs, q)
            gq_ref[:, at] = (dot(gs, k2, 0, 0) * score_scale).astype(BF16)
        gk_parts.append((gk[:keys, :HEAD_DIM] + gk[keys:, HEAD_DIM:]) * score_scale)
        gv_parts.append(gv[:keys, :HEAD_DIM] + gv[keys:, HEAD_DIM:])
    terms = jnp.concatenate([jnp.concatenate(gk_parts, 1), jnp.concatenate(gv_parts, 1)], 0).astype(BF16)
    terms_ref[...] = dot(pick, terms, 0, 0).astype(BF16)


def local(queries, keys, values, grad_out, block_map, block_count):
    spans, cores = lax.axis_size("seq"), lax.axis_size("vis")
    me = lax.axis_index("seq").astype(jnp.int32).reshape(1)
    per_owner, rows, columns = keys.shape
    heads = queries.shape[1] // HEAD_DIM
    width = max(heads // GROUP, 1) * HEAD_DIM
    starts = tuple(core * heads // GROUP * HEAD_DIM for core in range(cores))
    tokens = queries.shape[0]
    counts = block_count.reshape(spans, 1)
    flat = (per_owner * rows, columns)
    smem = pl.BlockSpec(memory_space=pltpu.SMEM)
    params = pltpu.CompilerParams(vmem_limit_bytes=32 * 1024 * 1024)

    sent = pl.pallas_call(
        functools.partial(send_kernel, width, starts, rows, per_owner),
        out_shape=jax.ShapeDtypeStruct((cores, spans * 2 * rows, width), BF16),
        in_specs=[smem, VMEM, VMEM, VMEM, VMEM],
        out_specs=VMEM,
        compiler_params=params,
        name="choose_blocks",
    )(me, block_map, counts, keys.reshape(flat), values.reshape(flat))
    got = lax.all_to_all(
        sent.reshape(cores * spans, 2 * rows, width), ("vis", "seq"), split_axis=0, concat_axis=0, tiled=True
    )
    grad_queries, log_totals, terms = pl.pallas_call(
        functools.partial(attend_kernel, rows, per_owner, cores, spans),
        out_shape=(
            jax.ShapeDtypeStruct(queries.shape, BF16),
            jax.ShapeDtypeStruct((heads, tokens), F32),
            jax.ShapeDtypeStruct((cores * spans * 2 * rows, width), BF16),
        ),
        in_specs=[smem] + [VMEM] * 5,
        out_specs=(VMEM, VMEM, VMEM),
        compiler_params=params,
        name="attend",
    )(me, block_map, counts, queries, grad_out, got.reshape(-1, width))
    back = lax.all_to_all(
        terms.reshape(cores * spans, 2 * rows, width), ("vis", "seq"), split_axis=0, concat_axis=0, tiled=True
    )
    grad_keys, grad_values = pl.pallas_call(
        functools.partial(sum_kernel, width, starts, rows, per_owner),
        out_shape=(jax.ShapeDtypeStruct(flat, BF16),) * 2,
        in_specs=[smem, VMEM, VMEM, VMEM],
        out_specs=(VMEM, VMEM),
        compiler_params=params,
        name="sum_blocks",
    )(me, block_map, counts, back.reshape(cores, -1, width))
    return (grad_queries, log_totals, grad_keys.reshape(keys.shape), grad_values.reshape(keys.shape))


def solution(mesh):
    in_specs = (
        P("seq", "vis"),
        P("seq", "vis", None),
        P("seq", "vis", None),
        P("seq", "vis"),
        P(),
        P(),
    )
    out_specs = (P("seq", "vis"), P("vis", "seq"), P("seq", "vis", None), P("seq", "vis", None))
    return jax.shard_map(local, mesh=mesh, in_specs=in_specs, out_specs=out_specs, check_vma=False)
```

```python
import functools
import math

import jax
import jax.numpy as jnp
from jax import lax
from jax.experimental import pallas as pl
from jax.experimental.pallas import tpu as pltpu
from jax.sharding import PartitionSpec as P

HEAD_DIM = 128
GROUP = 8
BF16 = jnp.bfloat16
F32 = jnp.float32
VMEM = pl.BlockSpec(memory_space=pltpu.VMEM)
HBM = pl.BlockSpec(memory_space=pltpu.HBM)
SMEM = pl.BlockSpec(memory_space=pltpu.SMEM)


def iota(shape, dim):
    return lax.broadcasted_iota(jnp.int32, shape, dim)


def dot(left, right, left_dim=1, right_dim=0):
    return lax.dot_general(
        left, right, (((left_dim,), (right_dim,)), ((), ())), preferred_element_type=F32
    )


def copy_all(pairs, sems):
    copies = [pltpu.make_async_copy(src, dst, sems.at[i]) for i, (src, dst) in enumerate(pairs)]
    for copy in copies:
        copy.start()
    for copy in copies:
        copy.wait()


def choose_kernel(
    width, starts, me_ref, map_hbm, count_hbm, keys_hbm, values_hbm, out_ref, pick_ref, map_ref, count_ref, keys_ref, values_ref, sems
):
    copy_all(
        ((map_hbm, map_ref), (count_hbm, count_ref), (keys_hbm, keys_ref), (values_hbm, values_ref)), sems
    )
    per_owner, rows, _ = keys_ref.shape
    most, spans = map_ref.shape
    block_map = map_ref[...]
    live = iota((most, spans), 0) < count_ref[...]
    asked = live & (block_map // per_owner == me_ref[0])
    slot = jnp.sum(jnp.where(asked, block_map % per_owner + 1, 0), axis=0, keepdims=True) - 1
    slot_rows, span_rows = pick_ref.shape
    expand = (iota((span_rows, spans), 0) // (2 * rows) == iota((span_rows, spans), 1)).astype(BF16)
    want = dot(jnp.broadcast_to(slot, (slot_rows, spans)).astype(F32).astype(BF16), expand, 1, 1)
    have, place = iota(pick_ref.shape, 0), iota(pick_ref.shape, 1) % (2 * rows)
    have_slot = have % (per_owner * rows) // rows
    have_place = have // (per_owner * rows) * rows + have % rows
    pick = ((want == have_slot.astype(F32)) & (place == have_place)).astype(BF16)
    pick_ref[...] = pick
    stacked = [ref[slot].astype(F32) for ref in (keys_ref, values_ref) for slot in range(per_owner)]
    stacked = jnp.concatenate(stacked, axis=0).astype(BF16)
    for core, start in enumerate(starts):
        out_ref[core] = dot(pick, stacked[:, start : start + width], 0, 0).astype(BF16)


def load_kernel(
    rows, per_owner, cores, me_ref, map_hbm, count_hbm, q_hbm, g_hbm, q_ref, g_ref, pick_ref, live_ref, map_ref, count_ref, sems
):
    copies = [pltpu.make_async_copy(src, dst, sems.at[2 + i]) for i, (src, dst) in enumerate(((q_hbm, q_ref), (g_hbm, g_ref)))]
    for copy in copies:
        copy.start()
    copy_all(((map_hbm, map_ref), (count_hbm, count_ref)), sems)
    most, spans = map_ref.shape
    block_rows = cores * rows
    keys = most * block_rows
    here = iota((1, spans), 1) == me_ref[0]
    owners = jnp.sum(jnp.where(here, map_ref[...] // per_owner, 0), axis=1, keepdims=True)
    count = jnp.sum(jnp.where(here, count_ref[...], 0), axis=1, keepdims=True)
    mine, theirs = iota((2 * keys, 1), 0), iota(pick_ref.shape, 1)
    block = mine % keys // block_rows
    expand = (iota((2 * keys, most), 1) == block).astype(BF16)
    lanes = 128
    owner = dot(expand, jnp.broadcast_to(owners, (most, lanes)).astype(F32).astype(BF16))[:, :1].astype(jnp.int32)
    place = ((mine % block_rows // rows * spans + owner) * 2 + mine // keys) * rows + mine % rows
    place = jnp.where(block < count, place, -1)
    pick_ref[...] = (place == theirs).astype(BF16)
    live_ref[...] = jnp.where(iota(live_ref.shape, 0) // block_rows < count, 0.0, -1e30)
    for copy in copies:
        copy.wait()


def block_diagonal(part):
    zero = jnp.zeros_like(part)
    return jnp.concatenate([jnp.concatenate([part, zero], 1), jnp.concatenate([zero, part], 1)], 0)


def attend_kernel(q_ref, g_ref, pick_ref, live_ref, rows_ref, terms_ref, gs_ref, k_ref, log_ref):
    score_scale = 1.0 / math.sqrt(HEAD_DIM)
    keys = k_ref.shape[0]
    kv_heads = k_ref.shape[1] // HEAD_DIM
    tokens = q_ref.shape[0]
    per_kv = q_ref.shape[1] // HEAD_DIM // kv_heads
    pick = pick_ref[...]
    fetched = dot(pick, rows_ref[...]).astype(BF16)
    k_ref[...] = fetched[:keys]
    live = live_ref[...]

    gk_parts, gv_parts = [], []
    for kv in range(kv_heads):
        cols = slice(kv * HEAD_DIM, (kv + 1) * HEAD_DIM)
        k2, v2 = block_diagonal(fetched[:keys, cols]), block_diagonal(fetched[keys:, cols])
        gk = jnp.zeros((2 * keys, 2 * HEAD_DIM), F32)
        gv = jnp.zeros((2 * keys, 2 * HEAD_DIM), F32)
        for pair in range(per_kv // 2):
            head = kv * per_kv + 2 * pair
            at = slice(head * HEAD_DIM, (head + 2) * HEAD_DIM)
            q, g = q_ref[:, at], g_ref[:, at]
            scores = (dot(k2, q, 1, 1) * score_scale).reshape(2, keys, tokens) + live
            row_max = jnp.max(scores, axis=1, keepdims=True)
            weights = jnp.exp(scores - row_max)
            totals = jnp.sum(weights, axis=1, keepdims=True)
            probs = weights * (1.0 / totals)
            log_ref[head : head + 2, :] = (row_max + jnp.log(totals)).reshape(2, tokens)
            low = probs.astype(BF16)
            grad_probs = dot(v2, g, 1, 1).reshape(2, keys, tokens)
            delta = jnp.sum(low.astype(F32) * grad_probs, axis=1, keepdims=True)
            gs = (probs * (grad_probs - delta)).astype(BF16).reshape(2 * keys, tokens)
            gs_ref[head // 2] = gs
            gv += dot(low.reshape(2 * keys, tokens), g)
            gk += dot(gs, q)
        gk_parts.append((gk[:keys, :HEAD_DIM] + gk[keys:, HEAD_DIM:]) * score_scale)
        gv_parts.append(gv[:keys, :HEAD_DIM] + gv[keys:, HEAD_DIM:])
    terms = jnp.concatenate([jnp.concatenate(gk_parts, 1), jnp.concatenate(gv_parts, 1)], 0).astype(BF16)
    terms_ref[...] = dot(pick, terms, 0, 0).astype(BF16)


def queries_kernel(gs_ref, k_ref, log_ref, out_hbm, log_hbm, out_ref, sems):
    score_scale = 1.0 / math.sqrt(HEAD_DIM)
    pairs = gs_ref.shape[0]
    kv_heads = k_ref.shape[1] // HEAD_DIM
    copies = [pltpu.make_async_copy(log_ref, log_hbm, sems.at[pairs])]
    copies[0].start()
    for kv in range(kv_heads):
        k2 = block_diagonal(k_ref[:, kv * HEAD_DIM : (kv + 1) * HEAD_DIM])
        for pair in range(kv * pairs // kv_heads, (kv + 1) * pairs // kv_heads):
            at = slice(2 * pair * HEAD_DIM, 2 * (pair + 1) * HEAD_DIM)
            out_ref[:, at] = (dot(gs_ref[pair], k2, 0, 0) * score_scale).astype(BF16)
            copies.append(pltpu.make_async_copy(out_ref.at[:, at], out_hbm.at[:, at], sems.at[pair]))
            copies[-1].start()
    for copy in copies:
        copy.wait()


def sum_kernel(width, starts, pick_ref, terms_ref, keys_ref, values_ref):
    per_owner, rows, _ = keys_ref.shape
    done = {}
    for core, start in enumerate(starts):
        part = dot(pick_ref[...], terms_ref[core])
        done[start] = done[start] + part if start in done else part
    for start, total in done.items():
        for slot in range(per_owner):
            for place, ref in ((slot, keys_ref), (per_owner + slot, values_ref)):
                ref[slot, :, start : start + width] = total[place * rows : (place + 1) * rows].astype(BF16)


def local(queries, keys, values, grad_out, block_map, block_count):
    spans, cores = lax.axis_size("seq"), lax.axis_size("vis")
    me = lax.axis_index("seq").astype(jnp.int32).reshape(1)
    per_owner, rows, _ = keys.shape
    tokens = queries.shape[0]
    heads = queries.shape[1] // HEAD_DIM
    most = block_map.shape[1]
    width = max(heads // GROUP, 1) * HEAD_DIM
    starts = tuple(core * heads // GROUP * HEAD_DIM for core in range(cores))
    attended = most * cores * rows
    block_map = block_map.T
    block_count = block_count.reshape(1, spans)
    stay = functools.partial(pltpu.with_memory_space_constraint, memory_space=pltpu.HBM)
    shape = jax.ShapeDtypeStruct
    params = pltpu.CompilerParams(vmem_limit_bytes=24 * 1024 * 1024)
    table_scratch = [pltpu.VMEM((most, spans), jnp.int32), pltpu.VMEM((1, spans), jnp.int32)]

    sent, pick = pl.pallas_call(
        functools.partial(choose_kernel, width, starts),
        out_shape=(
            shape((cores, spans * 2 * rows, width), BF16),
            shape((2 * per_owner * rows, spans * 2 * rows), BF16),
        ),
        in_specs=[SMEM, HBM, HBM, HBM, HBM],
        out_specs=(VMEM, VMEM),
        scratch_shapes=table_scratch
        + [pltpu.VMEM(keys.shape, BF16), pltpu.VMEM(keys.shape, BF16), pltpu.SemaphoreType.DMA((4,))],
        compiler_params=params,
        name="choose_blocks",
    )(me, stay(block_map), stay(block_count), stay(keys), stay(values))
    got = lax.all_to_all(
        sent.reshape(cores * spans, 2 * rows, width), ("vis", "seq"), split_axis=0, concat_axis=0, tiled=True
    )
    q, g, order, live = pl.pallas_call(
        functools.partial(load_kernel, rows, per_owner, cores),
        out_shape=(
            shape(queries.shape, BF16),
            shape(queries.shape, BF16),
            shape((2 * attended, cores * spans * 2 * rows), BF16),
            shape((attended, tokens), F32),
        ),
        in_specs=[SMEM, HBM, HBM, HBM, HBM],
        out_specs=(VMEM,) * 4,
        scratch_shapes=table_scratch + [pltpu.SemaphoreType.DMA((4,))],
        compiler_params=params,
        cost_estimate=pl.CostEstimate(flops=10**6, bytes_accessed=2 * queries.size * 4, transcendentals=0),
        name="load_operands",
    )(me, stay(block_map), stay(block_count), stay(queries), stay(grad_out))
    terms, gs, k, logs = pl.pallas_call(
        attend_kernel,
        out_shape=(
            shape((cores * spans * 2 * rows, width), BF16),
            shape((heads // 2, 2 * attended, tokens), BF16),
            shape((attended, width), BF16),
            shape((heads, tokens), F32),
        ),
        in_specs=[VMEM] * 5,
        out_specs=(VMEM,) * 4,
        compiler_params=params,
        name="attend",
    )(q, g, order, live, got.reshape(-1, width))
    back = lax.all_to_all(
        terms.reshape(cores * spans, 2 * rows, width), ("vis", "seq"), split_axis=0, concat_axis=0, tiled=True
    )
    grad_queries, log_totals = pl.pallas_call(
        queries_kernel,
        out_shape=(shape(queries.shape, BF16), shape((heads, tokens), F32)),
        in_specs=[VMEM] * 3,
        out_specs=(HBM, HBM),
        scratch_shapes=[pltpu.VMEM(queries.shape, BF16), pltpu.SemaphoreType.DMA((heads // 2 + 1,))],
        compiler_params=params,
        cost_estimate=pl.CostEstimate(
            flops=4 * tokens * attended * heads * HEAD_DIM, bytes_accessed=4 * queries.size, transcendentals=0
        ),
        name="grad_queries",
    )(gs, k, logs)
    grad_keys, grad_values = pl.pallas_call(
        functools.partial(sum_kernel, width, starts),
        out_shape=(shape(keys.shape, BF16),) * 2,
        in_specs=[VMEM, VMEM],
        out_specs=(VMEM, VMEM),
        compiler_params=params,
        name="sum_blocks",
    )(pick, back.reshape(cores, -1, width))
    return grad_queries, log_totals, grad_keys, grad_values


def solution(mesh):
    in_specs = (
        P("seq", "vis"),
        P("seq", "vis", None),
        P("seq", "vis", None),
        P("seq", "vis"),
        P(),
        P(),
    )
    out_specs = (P("seq", "vis"), P("vis", "seq"), P("seq", "vis", None), P("seq", "vis", None))
    return jax.shard_map(local, mesh=mesh, in_specs=in_specs, out_specs=out_specs, check_vma=False)
```

```python
import functools
import math

import jax
import jax.numpy as jnp
from jax import lax
from jax.experimental import pallas as pl
from jax.experimental.pallas import tpu as pltpu
from jax.sharding import PartitionSpec as P

HEAD_DIM = 128
GROUP = 8
BF16 = jnp.bfloat16
F32 = jnp.float32
LOG2E = math.log2(math.e)
VMEM = pl.BlockSpec(memory_space=pltpu.VMEM)
HBM = pl.BlockSpec(memory_space=pltpu.HBM)
SMEM = pl.BlockSpec(memory_space=pltpu.SMEM)


def iota(shape, dim):
    return lax.broadcasted_iota(jnp.int32, shape, dim)


def dot(left, right, left_dim=1, right_dim=0):
    return lax.dot_general(
        left, right, (((left_dim,), (right_dim,)), ((), ())), preferred_element_type=F32
    )


def choose_kernel(
    width, starts, me_ref, map_hbm, count_hbm, keys_hbm, values_hbm, q_hbm, g_hbm,
    out_ref, pick_ref, order_ref, live_ref, q_ref, g_ref, map_ref, count_ref, keys_ref, values_ref, sems
):
    pairs = (
        (map_hbm, map_ref), (count_hbm, count_ref), (keys_hbm, keys_ref), (values_hbm, values_ref), (q_hbm, q_ref), (g_hbm, g_ref)
    )
    copies = [pltpu.make_async_copy(src, dst, sems.at[i]) for i, (src, dst) in enumerate(pairs)]
    for copy in copies:
        copy.start()
    me = me_ref[0]
    per_owner, rows, _ = keys_ref.shape
    most, spans = map_ref.shape
    cores = len(starts)

    slot_rows, span_rows = pick_ref.shape
    expand_spans = (iota((span_rows, spans), 0) // (2 * rows) == iota((span_rows, spans), 1)).astype(BF16)
    have, place = iota((slot_rows, 1), 0), iota((1, span_rows), 1) % (2 * rows)
    have_slot = (have % (per_owner * rows) // rows + 1).astype(F32)
    have_place = have // (per_owner * rows) * rows + have % rows
    same_place = have_place == place

    block_rows = cores * rows
    keys = most * block_rows
    mine, theirs = iota((2 * keys, 1), 0), iota(order_ref.shape, 1)
    block = mine % keys // block_rows
    expand_blocks = (iota((2 * keys, most), 1) == block).astype(BF16)
    offset = mine % block_rows // rows * (spans * 2 * rows) + mine // keys * rows + mine % rows
    here = iota((1, spans), 1) == me
    live_block = iota(live_ref.shape, 0) // block_rows

    for copy in copies[:4]:
        copy.wait()
    relative = map_ref[...] - me * per_owner
    asked = (relative >= 0) & (relative < per_owner) & (iota((most, spans), 0) < count_ref[...])
    slot = jnp.sum(jnp.where(asked, relative + 1, 0), axis=0, keepdims=True).astype(F32)
    want = dot(jnp.broadcast_to(slot, (slot_rows, spans)).astype(BF16), expand_spans, 1, 1)
    pick = ((want == have_slot) & same_place).astype(BF16)
    stacked = [ref[slot].astype(F32) for ref in (keys_ref, values_ref) for slot in range(per_owner)]
    stacked = jnp.concatenate(stacked, axis=0).astype(BF16)
    for core, start in enumerate(starts):
        out_ref[core] = dot(pick, stacked[:, start : start + width], 0, 0).astype(BF16)
    pick_ref[...] = pick

    owners = jnp.sum(jnp.where(here, map_ref[...] // per_owner, 0), axis=1, keepdims=True)
    count = jnp.sum(jnp.where(here, count_ref[...], 0), axis=1, keepdims=True)
    lanes = jnp.broadcast_to(owners.astype(F32), (most, order_ref.shape[1])).astype(BF16)
    owner = dot(expand_blocks, lanes).astype(jnp.int32)
    travels = jnp.where(block < count, offset, -theirs.shape[1] * most * spans) + owner * (2 * rows)
    order_ref[...] = (travels == theirs).astype(BF16)
    live_ref[...] = jnp.where(live_block < count, 0.0, -1e30)
    for copy in copies[4:]:
        copy.wait()


def block_diagonal(part):
    zero = jnp.zeros_like(part)
    return jnp.concatenate([jnp.concatenate([part, zero], 1), jnp.concatenate([zero, part], 1)], 0)


def attend_kernel(
    q_ref, g_ref, order_ref, live_ref, rows_ref, terms_ref, gq_hbm, log_hbm,
    scores_ref, gp_ref, probs_ref, low_ref, gs_ref, gq_ref, log_ref, sems
):
    score_scale = 1.0 / math.sqrt(HEAD_DIM)
    keys, tokens = live_ref.shape
    kv_heads = rows_ref.shape[1] // HEAD_DIM
    pairs = gs_ref.shape[0]
    split, joined = (2, keys, tokens), (2 * keys, tokens)
    columns = [slice(2 * pair * HEAD_DIM, 2 * (pair + 1) * HEAD_DIM) for pair in range(pairs)]
    order, live = order_ref[...], live_ref[...]
    fetched = dot(order, rows_ref[...]).astype(BF16)
    heads = [fetched[:, kv * HEAD_DIM : (kv + 1) * HEAD_DIM] for kv in range(kv_heads)]
    k2 = [block_diagonal(head[:keys]) for head in heads for _ in range(pairs // kv_heads)]
    v2 = [block_diagonal(head[keys:]) for head in heads for _ in range(pairs // kv_heads)]

    for pair, at in enumerate(columns):
        scores_ref[pair] = dot(k2[pair], q_ref[:, at], 1, 1)
    for pair in range(pairs):
        scores = scores_ref[pair].reshape(split) * (score_scale * LOG2E) + live
        row_max = jnp.max(scores, axis=1, keepdims=True)
        weights = jnp.exp2(scores - row_max)
        totals = jnp.sum(weights, axis=1, keepdims=True)
        probs = weights * (1.0 / totals)
        log_ref[2 * pair : 2 * pair + 2, :] = ((row_max + jnp.log2(totals)) * (1.0 / LOG2E)).reshape(2, tokens)
        probs_ref[pair] = probs.reshape(joined)
        low_ref[pair] = probs.astype(BF16).reshape(joined)
    copies = [pltpu.make_async_copy(log_ref, log_hbm, sems.at[pairs])]
    copies[0].start()
    for pair, at in enumerate(columns):
        gp_ref[pair] = dot(v2[pair], g_ref[:, at], 1, 1)
    for pair in range(pairs):
        grad_probs = gp_ref[pair].reshape(split)
        delta = jnp.sum(low_ref[pair].reshape(split).astype(F32) * grad_probs, axis=1, keepdims=True)
        gs_ref[pair] = (probs_ref[pair].reshape(split) * (grad_probs - delta)).astype(BF16).reshape(joined)
    for pair, at in enumerate(columns):
        gq_ref[:, at] = (dot(gs_ref[pair], k2[pair], 0, 0) * score_scale).astype(BF16)
        copies.append(pltpu.make_async_copy(gq_ref.at[:, at], gq_hbm.at[:, at], sems.at[pair]))
        copies[-1].start()
    gk, gv = [0.0] * kv_heads, [0.0] * kv_heads
    for pair, at in enumerate(columns):
        kv = pair * kv_heads // pairs
        gk[kv] += dot(gs_ref[pair], q_ref[:, at])
        gv[kv] += dot(low_ref[pair], g_ref[:, at])
    gk = [(part[:keys, :HEAD_DIM] + part[keys:, HEAD_DIM:]) * score_scale for part in gk]
    gv = [part[:keys, :HEAD_DIM] + part[keys:, HEAD_DIM:] for part in gv]
    terms = jnp.concatenate([jnp.concatenate(gk, 1), jnp.concatenate(gv, 1)], 0).astype(BF16)
    terms_ref[...] = dot(order, terms, 0, 0).astype(BF16)
    for copy in copies:
        copy.wait()


def sum_kernel(width, starts, pick_ref, terms_ref, keys_ref, values_ref):
    per_owner, rows, _ = keys_ref.shape
    done = {}
    for core, start in enumerate(starts):
        part = dot(pick_ref[...], terms_ref[core])
        done[start] = done[start] + part if start in done else part
    for start, total in done.items():
        for slot in range(per_owner):
            for place, ref in ((slot, keys_ref), (per_owner + slot, values_ref)):
                ref[slot, :, start : start + width] = total[place * rows : (place + 1) * rows].astype(BF16)


def local(queries, keys, values, grad_out, block_map, block_count):
    spans, cores = lax.axis_size("seq"), lax.axis_size("vis")
    me = lax.axis_index("seq").astype(jnp.int32).reshape(1)
    per_owner, rows, _ = keys.shape
    tokens = queries.shape[0]
    heads = queries.shape[1] // HEAD_DIM
    most = block_map.shape[1]
    width = max(heads // GROUP, 1) * HEAD_DIM
    starts = tuple(core * heads // GROUP * HEAD_DIM for core in range(cores))
    attended = most * cores * rows
    travelling = spans * 2 * rows
    shape = jax.ShapeDtypeStruct
    params = pltpu.CompilerParams(vmem_limit_bytes=24 * 1024 * 1024)
    stay = functools.partial(pltpu.with_memory_space_constraint, memory_space=pltpu.HBM)

    sent, pick, order, live, q, g = pl.pallas_call(
        functools.partial(choose_kernel, width, starts),
        out_shape=(
            shape((cores, travelling, width), BF16),
            shape((2 * per_owner * rows, travelling), BF16),
            shape((2 * attended, cores * travelling), BF16),
            shape((attended, tokens), F32),
            shape(queries.shape, BF16),
            shape(queries.shape, BF16),
        ),
        in_specs=[SMEM] + [HBM] * 6,
        out_specs=(VMEM,) * 6,
        scratch_shapes=[
            pltpu.VMEM((most, spans), jnp.int32),
            pltpu.VMEM((1, spans), jnp.int32),
            pltpu.VMEM(keys.shape, BF16),
            pltpu.VMEM(keys.shape, BF16),
            pltpu.SemaphoreType.DMA((6,)),
        ],
        compiler_params=params,
        name="choose_blocks",
    )(me, *map(stay, (block_map.T, block_count.reshape(1, spans), keys, values, queries, grad_out)))
    got = lax.all_to_all(
        sent.reshape(cores * spans, 2 * rows, width), ("vis", "seq"), split_axis=0, concat_axis=0, tiled=True
    )
    pair_shape = (heads // 2, 2 * attended, tokens)
    terms, grad_queries, log_totals = pl.pallas_call(
        attend_kernel,
        out_shape=(
            shape((cores * travelling, width), BF16),
            shape(queries.shape, BF16),
            shape((heads, tokens), F32),
        ),
        in_specs=[VMEM] * 5,
        out_specs=(VMEM, HBM, HBM),
        scratch_shapes=[pltpu.VMEM(pair_shape, kind) for kind in (F32, F32, F32, BF16, BF16)]
        + [
            pltpu.VMEM(queries.shape, BF16),
            pltpu.VMEM((heads, tokens), F32),
            pltpu.SemaphoreType.DMA((heads // 2 + 1,)),
        ],
        compiler_params=params,
        name="attend",
    )(q, g, order, live, got.reshape(-1, width))
    back = lax.all_to_all(
        terms.reshape(cores * spans, 2 * rows, width), ("vis", "seq"), split_axis=0, concat_axis=0, tiled=True
    )
    grad_keys, grad_values = pl.pallas_call(
        functools.partial(sum_kernel, width, starts),
        out_shape=(shape(keys.shape, BF16),) * 2,
        in_specs=[VMEM, VMEM],
        out_specs=(VMEM, VMEM),
        compiler_params=params,
        name="sum_blocks",
    )(pick, back.reshape(cores, -1, width))
    return grad_queries, log_totals, grad_keys, grad_values


def solution(mesh):
    in_specs = (
        P("seq", "vis"),
        P("seq", "vis", None),
        P("seq", "vis", None),
        P("seq", "vis"),
        P(),
        P(),
    )
    out_specs = (P("seq", "vis"), P("vis", "seq"), P("seq", "vis", None), P("seq", "vis", None))
    return jax.shard_map(local, mesh=mesh, in_specs=in_specs, out_specs=out_specs, check_vma=False)
```

```python
import functools
import math

import jax
import jax.numpy as jnp
from jax import lax
from jax.experimental import pallas as pl
from jax.experimental.pallas import tpu as pltpu
from jax.sharding import PartitionSpec as P

HEAD_DIM = 128
GROUP = 8
BF16 = jnp.bfloat16
F32 = jnp.float32
LOG2E = math.log2(math.e)
VMEM = pl.BlockSpec(memory_space=pltpu.VMEM)
HBM = pl.BlockSpec(memory_space=pltpu.HBM)
SMEM = pl.BlockSpec(memory_space=pltpu.SMEM)


def iota(shape, dim):
    return lax.broadcasted_iota(jnp.int32, shape, dim)


def dot(left, right, left_dim=1, right_dim=0):
    return lax.dot_general(
        left, right, (((left_dim,), (right_dim,)), ((), ())), preferred_element_type=F32
    )


def choose_kernel(
    width, starts, me_ref, map_hbm, count_hbm, keys_hbm, values_hbm, q_hbm, g_hbm,
    out_ref, pick_ref, order_ref, live_ref, q_ref, g_ref, map_ref, count_ref, keys_ref, values_ref, sems
):
    pairs = (
        (map_hbm, map_ref), (count_hbm, count_ref), (keys_hbm, keys_ref), (values_hbm, values_ref), (q_hbm, q_ref), (g_hbm, g_ref)
    )
    copies = [pltpu.make_async_copy(src, dst, sems.at[i]) for i, (src, dst) in enumerate(pairs)]
    for copy in copies:
        copy.start()
    me = me_ref[0]
    per_owner, rows, _ = keys_ref.shape
    most, spans = map_ref.shape
    cores = len(starts)

    slot_rows, span_rows = pick_ref.shape
    expand_spans = (iota((span_rows, spans), 0) // (2 * rows) == iota((span_rows, spans), 1)).astype(BF16)
    have, place = iota((slot_rows, 1), 0), iota((1, span_rows), 1) % (2 * rows)
    have_slot = (have % (per_owner * rows) // rows + 1).astype(F32)
    have_place = have // (per_owner * rows) * rows + have % rows
    same_place = have_place == place

    block_rows = cores * rows
    keys = most * block_rows
    mine, theirs = iota((2 * keys, 1), 0), iota(order_ref.shape, 1)
    block = mine % keys // block_rows
    expand_blocks = (iota((2 * keys, most), 1) == block).astype(BF16)
    offset = mine % block_rows // rows * (spans * 2 * rows) + mine // keys * rows + mine % rows
    here = iota((1, spans), 1) == me
    live_block = iota(live_ref.shape, 0) // block_rows

    for copy in copies[:4]:
        copy.wait()
    relative = map_ref[...] - me * per_owner
    asked = (relative >= 0) & (relative < per_owner) & (iota((most, spans), 0) < count_ref[...])
    slot = jnp.sum(jnp.where(asked, relative + 1, 0), axis=0, keepdims=True).astype(F32)
    want = dot(jnp.broadcast_to(slot, (slot_rows, spans)).astype(BF16), expand_spans, 1, 1)
    pick = ((want == have_slot) & same_place).astype(BF16)
    stacked = [ref[slot].astype(F32) for ref in (keys_ref, values_ref) for slot in range(per_owner)]
    stacked = jnp.concatenate(stacked, axis=0).astype(BF16)
    for core, start in enumerate(starts):
        out_ref[core] = dot(pick, stacked[:, start : start + width], 0, 0).astype(BF16)
    pick_ref[...] = pick

    owners = jnp.sum(jnp.where(here, map_ref[...] // per_owner, 0), axis=1, keepdims=True)
    count = jnp.sum(jnp.where(here, count_ref[...], 0), axis=1, keepdims=True)
    lanes = jnp.broadcast_to(owners.astype(F32), (most, order_ref.shape[1])).astype(BF16)
    owner = dot(expand_blocks, lanes).astype(jnp.int32)
    travels = jnp.where(block < count, offset, -theirs.shape[1] * most * spans) + owner * (2 * rows)
    order_ref[...] = (travels == theirs).astype(BF16)
    live_ref[...] = jnp.where(live_block < count, 0.0, -1e30)
    for copy in copies[4:]:
        copy.wait()


def block_diagonal(part):
    zero = jnp.zeros_like(part)
    return jnp.concatenate([jnp.concatenate([part, zero], 1), jnp.concatenate([zero, part], 1)], 0)


def grad_queries_of(pair, gs_ref, k2, gq_ref, gq_hbm, sem):
    score_scale = 1.0 / math.sqrt(HEAD_DIM)
    at = slice(2 * pair * HEAD_DIM, 2 * (pair + 1) * HEAD_DIM)
    gq_ref[:, at] = (dot(gs_ref[pair], k2, 0, 0) * score_scale).astype(BF16)
    copy = pltpu.make_async_copy(gq_ref.at[:, at], gq_hbm.at[:, at], sem)
    copy.start()
    return copy


def attend_body(
    early, q_ref, g_ref, order_ref, live_ref, rows_ref, terms_ref, gq_hbm, log_ref, gs_ref, k_ref,
    scores_ref, gp_ref, probs_ref, low_ref, gq_ref, sems
):
    score_scale = 1.0 / math.sqrt(HEAD_DIM)
    keys, tokens = live_ref.shape
    kv_heads = rows_ref.shape[1] // HEAD_DIM
    pairs = gs_ref.shape[0]
    split, joined = (2, keys, tokens), (2 * keys, tokens)
    columns = [slice(2 * pair * HEAD_DIM, 2 * (pair + 1) * HEAD_DIM) for pair in range(pairs)]
    order, live = order_ref[...], live_ref[...]
    fetched = dot(order, rows_ref[...]).astype(BF16)
    k_ref[...] = fetched[:keys]
    heads = [fetched[:, kv * HEAD_DIM : (kv + 1) * HEAD_DIM] for kv in range(kv_heads)]
    k2 = [block_diagonal(head[:keys]) for head in heads for _ in range(pairs // kv_heads)]
    v2 = [block_diagonal(head[keys:]) for head in heads for _ in range(pairs // kv_heads)]

    for pair, at in enumerate(columns):
        scores_ref[pair] = dot(k2[pair], q_ref[:, at], 1, 1)
    for pair in range(pairs):
        scores = scores_ref[pair].reshape(split) * (score_scale * LOG2E) + live
        row_max = jnp.max(scores, axis=1, keepdims=True)
        weights = jnp.exp2(scores - row_max)
        totals = jnp.sum(weights, axis=1, keepdims=True)
        probs = weights * (1.0 / totals)
        log_ref[2 * pair : 2 * pair + 2, :] = ((row_max + jnp.log2(totals)) * (1.0 / LOG2E)).reshape(2, tokens)
        probs_ref[pair] = probs.reshape(joined)
        low_ref[pair] = probs.astype(BF16).reshape(joined)
    copies = []
    for pair, at in enumerate(columns):
        gp_ref[pair] = dot(v2[pair], g_ref[:, at], 1, 1)
    for pair in range(pairs):
        grad_probs = gp_ref[pair].reshape(split)
        delta = jnp.sum(low_ref[pair].reshape(split).astype(F32) * grad_probs, axis=1, keepdims=True)
        gs_ref[pair] = (probs_ref[pair].reshape(split) * (grad_probs - delta)).astype(BF16).reshape(joined)
    if early:
        for pair in range(pairs):
            copies.append(grad_queries_of(pair, gs_ref, k2[pair], gq_ref, gq_hbm, sems.at[pair]))
    gk, gv = [0.0] * kv_heads, [0.0] * kv_heads
    for pair, at in enumerate(columns):
        kv = pair * kv_heads // pairs
        gk[kv] += dot(gs_ref[pair], q_ref[:, at])
        gv[kv] += dot(low_ref[pair], g_ref[:, at])
    gk = [(part[:keys, :HEAD_DIM] + part[keys:, HEAD_DIM:]) * score_scale for part in gk]
    gv = [part[:keys, :HEAD_DIM] + part[keys:, HEAD_DIM:] for part in gv]
    terms = jnp.concatenate([jnp.concatenate(gk, 1), jnp.concatenate(gv, 1)], 0).astype(BF16)
    terms_ref[...] = dot(order, terms, 0, 0).astype(BF16)
    for copy in copies:
        copy.wait()


def attend_kernel(me_ref, *refs):
    pl.when(me_ref[0] == 0)(lambda: attend_body(True, *refs))
    pl.when(me_ref[0] != 0)(lambda: attend_body(False, *refs))


def sum_kernel(
    width, starts, me_ref, pick_ref, terms_ref, gs_ref, k_ref, log_ref, _, keys_hbm, values_hbm, log_hbm, gq_hbm,
    keys_ref, values_ref, gq_ref, sems
):
    per_owner, rows, _ = keys_ref.shape
    done = {}
    for core, start in enumerate(starts):
        part = dot(pick_ref[...], terms_ref[core])
        done[start] = done[start] + part if start in done else part
    for start, total in done.items():
        for slot in range(per_owner):
            for place, ref in ((slot, keys_ref), (per_owner + slot, values_ref)):
                ref[slot, :, start : start + width] = total[place * rows : (place + 1) * rows].astype(BF16)
    pairs = gs_ref.shape[0]
    copies = [
        pltpu.make_async_copy(keys_ref, keys_hbm, sems.at[pairs]),
        pltpu.make_async_copy(values_ref, values_hbm, sems.at[pairs + 1]),
        pltpu.make_async_copy(log_ref, log_hbm, sems.at[pairs + 2]),
    ]
    for copy in copies:
        copy.start()

    @pl.when(me_ref[0] != 0)
    def _():
        kv_heads = k_ref.shape[1] // HEAD_DIM
        k2 = [block_diagonal(k_ref[:, kv * HEAD_DIM : (kv + 1) * HEAD_DIM]) for kv in range(kv_heads)]
        late = [
            grad_queries_of(pair, gs_ref, k2[pair * kv_heads // pairs], gq_ref, gq_hbm, sems.at[pair])
            for pair in range(pairs)
        ]
        for copy in late:
            copy.wait()

    for copy in copies:
        copy.wait()


def local(queries, keys, values, grad_out, block_map, block_count):
    spans, cores = lax.axis_size("seq"), lax.axis_size("vis")
    me = lax.axis_index("seq").astype(jnp.int32).reshape(1)
    per_owner, rows, _ = keys.shape
    tokens = queries.shape[0]
    heads = queries.shape[1] // HEAD_DIM
    most = block_map.shape[1]
    width = max(heads // GROUP, 1) * HEAD_DIM
    starts = tuple(core * heads // GROUP * HEAD_DIM for core in range(cores))
    attended = most * cores * rows
    travelling = spans * 2 * rows
    shape = jax.ShapeDtypeStruct
    params = pltpu.CompilerParams(vmem_limit_bytes=24 * 1024 * 1024)
    stay = functools.partial(pltpu.with_memory_space_constraint, memory_space=pltpu.HBM)

    sent, pick, order, live, q, g = pl.pallas_call(
        functools.partial(choose_kernel, width, starts),
        out_shape=(
            shape((cores, travelling, width), BF16),
            shape((2 * per_owner * rows, travelling), BF16),
            shape((2 * attended, cores * travelling), BF16),
            shape((attended, tokens), F32),
            shape(queries.shape, BF16),
            shape(queries.shape, BF16),
        ),
        in_specs=[SMEM] + [HBM] * 6,
        out_specs=(VMEM,) * 6,
        scratch_shapes=[
            pltpu.VMEM((most, spans), jnp.int32),
            pltpu.VMEM((1, spans), jnp.int32),
            pltpu.VMEM(keys.shape, BF16),
            pltpu.VMEM(keys.shape, BF16),
            pltpu.SemaphoreType.DMA((6,)),
        ],
        compiler_params=params,
        name="choose_blocks",
    )(me, *map(stay, (block_map.T, block_count.reshape(1, spans), keys, values, queries, grad_out)))
    got = lax.all_to_all(
        sent.reshape(cores * spans, 2 * rows, width), ("vis", "seq"), split_axis=0, concat_axis=0, tiled=True
    )
    pair_shape = (heads // 2, 2 * attended, tokens)
    terms, grad_queries, logs, gs, k = pl.pallas_call(
        attend_kernel,
        out_shape=(
            shape((cores * travelling, width), BF16),
            shape(queries.shape, BF16),
            shape((heads, tokens), F32),
            shape(pair_shape, BF16),
            shape((attended, width), BF16),
        ),
        in_specs=[SMEM] + [VMEM] * 5,
        out_specs=(VMEM, HBM, VMEM, VMEM, VMEM),
        scratch_shapes=[pltpu.VMEM(pair_shape, kind) for kind in (F32, F32, F32, BF16)]
        + [
            pltpu.VMEM(queries.shape, BF16),
            pltpu.SemaphoreType.DMA((heads // 2,)),
        ],
        compiler_params=params,
        name="attend",
    )(me, q, g, order, live, got.reshape(-1, width))
    back = lax.all_to_all(
        terms.reshape(cores * spans, 2 * rows, width), ("vis", "seq"), split_axis=0, concat_axis=0, tiled=True
    )
    grad_keys, grad_values, log_totals, grad_queries = pl.pallas_call(
        functools.partial(sum_kernel, width, starts),
        out_shape=(
            shape(keys.shape, BF16),
            shape(keys.shape, BF16),
            shape((heads, tokens), F32),
            shape(queries.shape, BF16),
        ),
        in_specs=[SMEM] + [VMEM] * 5 + [HBM],
        out_specs=(HBM,) * 4,
        scratch_shapes=[
            pltpu.VMEM(keys.shape, BF16),
            pltpu.VMEM(keys.shape, BF16),
            pltpu.VMEM(queries.shape, BF16),
            pltpu.SemaphoreType.DMA((heads // 2 + 3,)),
        ],
        input_output_aliases={6: 3},
        compiler_params=params,
        name="sum_blocks",
    )(me, pick, back.reshape(cores, -1, width), gs, k, logs, grad_queries)
    return grad_queries, log_totals, grad_keys, grad_values


def solution(mesh):
    in_specs = (
        P("seq", "vis"),
        P("seq", "vis", None),
        P("seq", "vis", None),
        P("seq", "vis"),
        P(),
        P(),
    )
    out_specs = (P("seq", "vis"), P("vis", "seq"), P("seq", "vis", None), P("seq", "vis", None))
    return jax.shard_map(local, mesh=mesh, in_specs=in_specs, out_specs=out_specs, check_vma=False)
```

```python
import functools
import math

import jax
import jax.numpy as jnp
import numpy as np
from jax import lax
from jax.experimental import pallas as pl
from jax.experimental.pallas import tpu as pltpu
from jax.sharding import PartitionSpec as P

HEAD_DIM = 128
GROUP = 8
BF16 = jnp.bfloat16
F32 = jnp.float32
LOG2E = math.log2(math.e)
VMEM = pl.BlockSpec(memory_space=pltpu.VMEM)
HBM = pl.BlockSpec(memory_space=pltpu.HBM)
SMEM = pl.BlockSpec(memory_space=pltpu.SMEM)
EXCHANGE_ORDER = {
    (16, 2): [18, 27, 28, 3, 6, 21, 13, 15, 22, 4, 12, 30, 7, 16, 23, 14, 20, 9, 17, 10, 29, 11, 0, 19, 26, 2, 24, 5, 1, 8, 31, 25],
}


def exchange_order(spans, cores):
    return EXCHANGE_ORDER.get((spans, cores)) or [span * cores + core for core in range(cores) for span in range(spans)]


def exchange(parts, order):
    return lax.all_to_all(
        parts, ("seq", "vis"), split_axis=0, concat_axis=0, tiled=True, axis_index_groups=[list(order)]
    )


def iota(shape, dim):
    return lax.broadcasted_iota(jnp.int32, shape, dim)


def dot(left, right, left_dim=1, right_dim=0):
    return lax.dot_general(
        left, right, (((left_dim,), (right_dim,)), ((), ())), preferred_element_type=F32
    )


def choose_kernel(
    starts, me_ref, map_hbm, count_hbm, place_hbm, keys_hbm, values_hbm, q_hbm, g_hbm,
    out_ref, pick_ref, order_ref, live_ref, q_ref, g_ref, map_ref, count_ref, place_ref, keys_ref, values_ref, sems
):
    pairs = (
        (map_hbm, map_ref), (count_hbm, count_ref), (place_hbm, place_ref), (keys_hbm, keys_ref), (values_hbm, values_ref), (q_hbm, q_ref), (g_hbm, g_ref)
    )
    copies = [pltpu.make_async_copy(src, dst, sems.at[i]) for i, (src, dst) in enumerate(pairs)]
    for copy in copies:
        copy.start()
    me = me_ref[0]
    per_owner, rows, _ = keys_ref.shape
    most, spans = map_ref.shape
    cores = len(starts)

    _, slot_rows, travelling = pick_ref.shape
    width = out_ref.shape[1]
    have, part = iota((slot_rows, 1), 0), iota((1, travelling), 1) % (2 * rows)
    have_slot = (have % (per_owner * rows) // rows + 1).astype(F32)
    same_part = have // (per_owner * rows) * rows + have % rows == part

    block_rows = cores * rows
    keys = most * block_rows
    mine = iota((2 * keys, 1), 0)
    block = mine % keys // block_rows
    expand_blocks = (iota((2 * keys, most), 1) == block).astype(BF16)
    same_row = mine // keys * rows + mine % rows == part
    core = mine % block_rows // rows
    here = iota((1, spans), 1) == me
    live_block = iota(live_ref.shape, 0) // block_rows

    for copy in copies[:5]:
        copy.wait()
    relative = map_ref[...] - me * per_owner
    asked = (relative >= 0) & (relative < per_owner) & (iota((most, spans), 0) < count_ref[...])
    slot = jnp.sum(jnp.where(asked, relative + 1, 0), axis=0, keepdims=True).astype(F32)
    place_span, place_core = place_ref[0:1, :], place_ref[1:2, :]
    expand_spans = (iota((spans, travelling), 0) == place_span).astype(BF16)
    want = dot(jnp.broadcast_to(slot, (slot_rows, spans)).astype(BF16), expand_spans)
    asked = (want == have_slot) & same_part
    stacked = [ref[slot].astype(F32) for ref in (keys_ref, values_ref) for slot in range(per_owner)]
    stacked = jnp.concatenate(stacked, axis=0).astype(BF16)
    out = 0.0
    for to, start in enumerate(starts):
        pick = (asked & (place_core == to)).astype(BF16)
        pick_ref[to] = pick
        out += dot(pick, stacked[:, start : start + width], 0, 0)
    out_ref[...] = out.astype(BF16)

    owners = jnp.sum(jnp.where(here, map_ref[...] // per_owner, 0), axis=1, keepdims=True)
    count = jnp.sum(jnp.where(here, count_ref[...], 0), axis=1, keepdims=True)
    lanes = jnp.broadcast_to(owners.astype(F32), (most, travelling)).astype(BF16)
    owner = dot(expand_blocks, lanes).astype(jnp.int32)
    order = same_row & (owner == place_span) & (core == place_core) & (block < count)
    order_ref[...] = order.astype(BF16)
    live_ref[...] = jnp.where(live_block < count, 0.0, -1e30)
    for copy in copies[5:]:
        copy.wait()


def block_diagonal(part):
    zero = jnp.zeros_like(part)
    return jnp.concatenate([jnp.concatenate([part, zero], 1), jnp.concatenate([zero, part], 1)], 0)


def grad_queries_of(pair, gs_ref, k2, gq_ref, gq_hbm, sem):
    score_scale = 1.0 / math.sqrt(HEAD_DIM)
    at = slice(2 * pair * HEAD_DIM, 2 * (pair + 1) * HEAD_DIM)
    gq_ref[:, at] = (dot(gs_ref[pair], k2, 0, 0) * score_scale).astype(BF16)
    copy = pltpu.make_async_copy(gq_ref.at[:, at], gq_hbm.at[:, at], sem)
    copy.start()
    return copy


def attend_body(
    early, q_ref, g_ref, order_ref, live_ref, rows_ref, terms_ref, gq_hbm, log_ref, gs_ref, k_ref,
    scores_ref, gp_ref, probs_ref, low_ref, gq_ref, sems
):
    score_scale = 1.0 / math.sqrt(HEAD_DIM)
    keys, tokens = live_ref.shape
    kv_heads = rows_ref.shape[1] // HEAD_DIM
    pairs = gs_ref.shape[0]
    split, joined = (2, keys, tokens), (2 * keys, tokens)
    columns = [slice(2 * pair * HEAD_DIM, 2 * (pair + 1) * HEAD_DIM) for pair in range(pairs)]
    order, live = order_ref[...], live_ref[...]
    fetched = dot(order, rows_ref[...]).astype(BF16)
    k_ref[...] = fetched[:keys]
    heads = [fetched[:, kv * HEAD_DIM : (kv + 1) * HEAD_DIM] for kv in range(kv_heads)]
    k2 = [block_diagonal(head[:keys]) for head in heads for _ in range(pairs // kv_heads)]
    v2 = [block_diagonal(head[keys:]) for head in heads for _ in range(pairs // kv_heads)]

    for pair, at in enumerate(columns):
        scores_ref[pair] = dot(k2[pair], q_ref[:, at], 1, 1)
    for pair in range(pairs):
        scores = scores_ref[pair].reshape(split) * (score_scale * LOG2E) + live
        row_max = jnp.max(scores, axis=1, keepdims=True)
        weights = jnp.exp2(scores - row_max)
        totals = jnp.sum(weights, axis=1, keepdims=True)
        probs = weights * (1.0 / totals)
        log_ref[2 * pair : 2 * pair + 2, :] = ((row_max + jnp.log2(totals)) * (1.0 / LOG2E)).reshape(2, tokens)
        probs_ref[pair] = probs.reshape(joined)
        low_ref[pair] = probs.astype(BF16).reshape(joined)
    copies = []
    for pair, at in enumerate(columns):
        gp_ref[pair] = dot(v2[pair], g_ref[:, at], 1, 1)
    for pair in range(pairs):
        grad_probs = gp_ref[pair].reshape(split)
        delta = jnp.sum(low_ref[pair].reshape(split).astype(F32) * grad_probs, axis=1, keepdims=True)
        gs_ref[pair] = (probs_ref[pair].reshape(split) * (grad_probs - delta)).astype(BF16).reshape(joined)
    if early:
        for pair in range(pairs):
            copies.append(grad_queries_of(pair, gs_ref, k2[pair], gq_ref, gq_hbm, sems.at[pair]))
    gk, gv = [0.0] * kv_heads, [0.0] * kv_heads
    for pair, at in enumerate(columns):
        kv = pair * kv_heads // pairs
        gk[kv] += dot(gs_ref[pair], q_ref[:, at])
        gv[kv] += dot(low_ref[pair], g_ref[:, at])
    gk = [(part[:keys, :HEAD_DIM] + part[keys:, HEAD_DIM:]) * score_scale for part in gk]
    gv = [part[:keys, :HEAD_DIM] + part[keys:, HEAD_DIM:] for part in gv]
    terms = jnp.concatenate([jnp.concatenate(gk, 1), jnp.concatenate(gv, 1)], 0).astype(BF16)
    terms_ref[...] = dot(order, terms, 0, 0).astype(BF16)
    for copy in copies:
        copy.wait()


def attend_kernel(me_ref, *refs):
    pl.when(me_ref[0] == 0)(lambda: attend_body(True, *refs))
    pl.when(me_ref[0] != 0)(lambda: attend_body(False, *refs))


def sum_kernel(
    starts, me_ref, pick_ref, terms_ref, gs_ref, k_ref, log_ref, _, keys_hbm, values_hbm, log_hbm, gq_hbm,
    keys_ref, values_ref, gq_ref, sems
):
    per_owner, rows, _ = keys_ref.shape
    width = terms_ref.shape[1]
    done = {}
    for core, start in enumerate(starts):
        part = dot(pick_ref[core], terms_ref[...])
        done[start] = done[start] + part if start in done else part
    for start, total in done.items():
        for slot in range(per_owner):
            for place, ref in ((slot, keys_ref), (per_owner + slot, values_ref)):
                ref[slot, :, start : start + width] = total[place * rows : (place + 1) * rows].astype(BF16)
    pairs = gs_ref.shape[0]
    copies = [
        pltpu.make_async_copy(keys_ref, keys_hbm, sems.at[pairs]),
        pltpu.make_async_copy(values_ref, values_hbm, sems.at[pairs + 1]),
        pltpu.make_async_copy(log_ref, log_hbm, sems.at[pairs + 2]),
    ]
    for copy in copies:
        copy.start()

    @pl.when(me_ref[0] != 0)
    def _():
        kv_heads = k_ref.shape[1] // HEAD_DIM
        k2 = [block_diagonal(k_ref[:, kv * HEAD_DIM : (kv + 1) * HEAD_DIM]) for kv in range(kv_heads)]
        late = [
            grad_queries_of(pair, gs_ref, k2[pair * kv_heads // pairs], gq_ref, gq_hbm, sems.at[pair])
            for pair in range(pairs)
        ]
        for copy in late:
            copy.wait()

    for copy in copies:
        copy.wait()


def local(queries, keys, values, grad_out, block_map, block_count):
    spans, cores = lax.axis_size("seq"), lax.axis_size("vis")
    me = lax.axis_index("seq").astype(jnp.int32).reshape(1)
    per_owner, rows, _ = keys.shape
    tokens = queries.shape[0]
    heads = queries.shape[1] // HEAD_DIM
    most = block_map.shape[1]
    width = max(heads // GROUP, 1) * HEAD_DIM
    starts = tuple(core * heads // GROUP * HEAD_DIM for core in range(cores))
    attended = most * cores * rows
    travelling = cores * spans * 2 * rows
    order_of = exchange_order(spans, cores)
    places = jnp.asarray(np.repeat(np.divmod(np.array(order_of, np.int32), cores), 2 * rows, axis=1))
    shape = jax.ShapeDtypeStruct
    params = pltpu.CompilerParams(vmem_limit_bytes=24 * 1024 * 1024)
    stay = functools.partial(pltpu.with_memory_space_constraint, memory_space=pltpu.HBM)

    sent, pick, order, live, q, g = pl.pallas_call(
        functools.partial(choose_kernel, starts),
        out_shape=(
            shape((travelling, width), BF16),
            shape((cores, 2 * per_owner * rows, travelling), BF16),
            shape((2 * attended, travelling), BF16),
            shape((attended, tokens), F32),
            shape(queries.shape, BF16),
            shape(queries.shape, BF16),
        ),
        in_specs=[SMEM] + [HBM] * 7,
        out_specs=(VMEM,) * 6,
        scratch_shapes=[
            pltpu.VMEM((most, spans), jnp.int32),
            pltpu.VMEM((1, spans), jnp.int32),
            pltpu.VMEM(places.shape, jnp.int32),
            pltpu.VMEM(keys.shape, BF16),
            pltpu.VMEM(keys.shape, BF16),
            pltpu.SemaphoreType.DMA((7,)),
        ],
        compiler_params=params,
        name="choose_blocks",
    )(me, *map(stay, (block_map.T, block_count.reshape(1, spans), places, keys, values, queries, grad_out)))
    got = exchange(sent.reshape(cores * spans, 2 * rows, width), order_of)
    pair_shape = (heads // 2, 2 * attended, tokens)
    terms, grad_queries, logs, gs, k = pl.pallas_call(
        attend_kernel,
        out_shape=(
            shape((travelling, width), BF16),
            shape(queries.shape, BF16),
            shape((heads, tokens), F32),
            shape(pair_shape, BF16),
            shape((attended, width), BF16),
        ),
        in_specs=[SMEM] + [VMEM] * 5,
        out_specs=(VMEM, HBM, VMEM, VMEM, VMEM),
        scratch_shapes=[pltpu.VMEM(pair_shape, kind) for kind in (F32, F32, F32, BF16)]
        + [
            pltpu.VMEM(queries.shape, BF16),
            pltpu.SemaphoreType.DMA((heads // 2,)),
        ],
        compiler_params=params,
        name="attend",
    )(me, q, g, order, live, got.reshape(-1, width))
    back = exchange(terms.reshape(cores * spans, 2 * rows, width), order_of)
    grad_keys, grad_values, log_totals, grad_queries = pl.pallas_call(
        functools.partial(sum_kernel, starts),
        out_shape=(
            shape(keys.shape, BF16),
            shape(keys.shape, BF16),
            shape((heads, tokens), F32),
            shape(queries.shape, BF16),
        ),
        in_specs=[SMEM] + [VMEM] * 5 + [HBM],
        out_specs=(HBM,) * 4,
        scratch_shapes=[
            pltpu.VMEM(keys.shape, BF16),
            pltpu.VMEM(keys.shape, BF16),
            pltpu.VMEM(queries.shape, BF16),
            pltpu.SemaphoreType.DMA((heads // 2 + 3,)),
        ],
        input_output_aliases={6: 3},
        compiler_params=params,
        name="sum_blocks",
    )(me, pick, back.reshape(-1, width), gs, k, logs, grad_queries)
    return grad_queries, log_totals, grad_keys, grad_values


def solution(mesh):
    in_specs = (
        P("seq", "vis"),
        P("seq", "vis", None),
        P("seq", "vis", None),
        P("seq", "vis"),
        P(),
        P(),
    )
    out_specs = (P("seq", "vis"), P("vis", "seq"), P("seq", "vis", None), P("seq", "vis", None))
    return jax.shard_map(local, mesh=mesh, in_specs=in_specs, out_specs=out_specs, check_vma=False)
```

```python
import functools
import math

import jax
import jax.numpy as jnp
import numpy as np
from jax import lax
from jax.experimental import pallas as pl
from jax.experimental.pallas import tpu as pltpu
from jax.sharding import PartitionSpec as P

HEAD_DIM = 128
GROUP = 8
BF16 = jnp.bfloat16
F32 = jnp.float32
LOG2E = math.log2(math.e)
VMEM = pl.BlockSpec(memory_space=pltpu.VMEM)
HBM = pl.BlockSpec(memory_space=pltpu.HBM)
SMEM = pl.BlockSpec(memory_space=pltpu.SMEM)
EXCHANGE_ORDER = {
    (16, 2): [18, 27, 28, 3, 6, 21, 13, 15, 22, 4, 12, 30, 7, 16, 23, 14, 20, 9, 17, 10, 29, 11, 0, 19, 26, 2, 24, 5, 1, 8, 31, 25],
}


def exchange_order(spans, cores):
    return EXCHANGE_ORDER.get((spans, cores)) or [span * cores + core for core in range(cores) for span in range(spans)]


def exchange(parts, order):
    return lax.all_to_all(
        parts, ("seq", "vis"), split_axis=0, concat_axis=0, tiled=True, axis_index_groups=[list(order)]
    )


def iota(shape, dim):
    return lax.broadcasted_iota(jnp.int32, shape, dim)


def dot(left, right, left_dim=1, right_dim=0):
    return lax.dot_general(
        left, right, (((left_dim,), (right_dim,)), ((), ())), preferred_element_type=F32
    )


def choose_kernel(
    starts, me_ref, map_hbm, count_hbm, place_hbm, keys_hbm, values_hbm,
    out_ref, pick_ref, order_ref, live_ref, map_ref, count_ref, place_ref, keys_ref, values_ref, sems
):
    pairs = (
        (map_hbm, map_ref), (count_hbm, count_ref), (place_hbm, place_ref), (keys_hbm, keys_ref), (values_hbm, values_ref)
    )
    copies = [pltpu.make_async_copy(src, dst, sems.at[i]) for i, (src, dst) in enumerate(pairs)]
    for copy in copies:
        copy.start()
    me = me_ref[0]
    per_owner, rows, _ = keys_ref.shape
    most, spans = map_ref.shape
    cores = len(starts)

    _, slot_rows, travelling = pick_ref.shape
    width = out_ref.shape[1]
    have, part = iota((slot_rows, 1), 0), iota((1, travelling), 1) % (2 * rows)
    have_slot = (have % (per_owner * rows) // rows + 1).astype(F32)
    same_part = have // (per_owner * rows) * rows + have % rows == part

    block_rows = cores * rows
    keys = most * block_rows
    mine = iota((2 * keys, 1), 0)
    block = mine % keys // block_rows
    expand_blocks = (iota((2 * keys, most), 1) == block).astype(BF16)
    same_row = mine // keys * rows + mine % rows == part
    core = mine % block_rows // rows
    here = iota((1, spans), 1) == me
    live_block = iota(live_ref.shape, 0) // block_rows

    for copy in copies:
        copy.wait()
    relative = map_ref[...] - me * per_owner
    asked = (relative >= 0) & (relative < per_owner) & (iota((most, spans), 0) < count_ref[...])
    slot = jnp.sum(jnp.where(asked, relative + 1, 0), axis=0, keepdims=True).astype(F32)
    place_span, place_core = place_ref[0:1, :], place_ref[1:2, :]
    expand_spans = (iota((spans, travelling), 0) == place_span).astype(BF16)
    want = dot(jnp.broadcast_to(slot, (slot_rows, spans)).astype(BF16), expand_spans)
    asked = (want == have_slot) & same_part
    stacked = [ref[slot].astype(F32) for ref in (keys_ref, values_ref) for slot in range(per_owner)]
    stacked = jnp.concatenate(stacked, axis=0).astype(BF16)
    out = 0.0
    for to, start in enumerate(starts):
        pick = (asked & (place_core == to)).astype(BF16)
        pick_ref[to] = pick
        out += dot(pick, stacked[:, start : start + width], 0, 0)
    out_ref[...] = out.astype(BF16)

    owners = jnp.sum(jnp.where(here, map_ref[...] // per_owner, 0), axis=1, keepdims=True)
    count = jnp.sum(jnp.where(here, count_ref[...], 0), axis=1, keepdims=True)
    lanes = jnp.broadcast_to(owners.astype(F32), (most, travelling)).astype(BF16)
    owner = dot(expand_blocks, lanes).astype(jnp.int32)
    order = same_row & (owner == place_span) & (core == place_core) & (block < count)
    order_ref[...] = order.astype(BF16)
    live_ref[...] = jnp.where(live_block < count, 0.0, -1e30)


def block_diagonal(part):
    zero = jnp.zeros_like(part)
    return jnp.concatenate([jnp.concatenate([part, zero], 1), jnp.concatenate([zero, part], 1)], 0)


def grad_queries_of(pair, gs_ref, k2, gq_ref, gq_hbm, sem):
    score_scale = 1.0 / math.sqrt(HEAD_DIM)
    at = slice(2 * pair * HEAD_DIM, 2 * (pair + 1) * HEAD_DIM)
    gq_ref[:, at] = (dot(gs_ref[pair], k2, 0, 0) * score_scale).astype(BF16)
    copy = pltpu.make_async_copy(gq_ref.at[:, at], gq_hbm.at[:, at], sem)
    copy.start()
    return copy


def attend_body(
    early, q_ref, g_ref, order_ref, live_ref, rows_ref, terms_ref, gq_hbm, log_ref, gs_ref, k_ref,
    scores_ref, gp_ref, probs_ref, low_ref, gq_ref, sems
):
    score_scale = 1.0 / math.sqrt(HEAD_DIM)
    keys, tokens = live_ref.shape
    kv_heads = rows_ref.shape[1] // HEAD_DIM
    pairs = gs_ref.shape[0]
    split, joined = (2, keys, tokens), (2 * keys, tokens)
    columns = [slice(2 * pair * HEAD_DIM, 2 * (pair + 1) * HEAD_DIM) for pair in range(pairs)]
    order, live = order_ref[...], live_ref[...]
    fetched = dot(order, rows_ref[...]).astype(BF16)
    k_ref[...] = fetched[:keys]
    heads = [fetched[:, kv * HEAD_DIM : (kv + 1) * HEAD_DIM] for kv in range(kv_heads)]
    k2 = [block_diagonal(head[:keys]) for head in heads for _ in range(pairs // kv_heads)]
    v2 = [block_diagonal(head[keys:]) for head in heads for _ in range(pairs // kv_heads)]

    copies = []
    gk, gv = [0.0] * kv_heads, [0.0] * kv_heads

    def score(pair):
        scores_ref[pair] = dot(k2[pair], q_ref[:, columns[pair]], 1, 1)

    def soften(pair):
        scores = scores_ref[pair].reshape(split) * (score_scale * LOG2E) + live
        row_max = jnp.max(scores, axis=1, keepdims=True)
        weights = jnp.exp2(scores - row_max)
        totals = jnp.sum(weights, axis=1, keepdims=True)
        probs = weights * (1.0 / totals)
        log_ref[2 * pair : 2 * pair + 2, :] = ((row_max + jnp.log2(totals)) * (1.0 / LOG2E)).reshape(2, tokens)
        probs_ref[pair] = probs.reshape(joined)
        low_ref[pair] = probs.astype(BF16).reshape(joined)

    def against_values(pair):
        gp_ref[pair] = dot(v2[pair], g_ref[:, columns[pair]], 1, 1)

    def grad_score(pair):
        grad_probs = gp_ref[pair].reshape(split)
        delta = jnp.sum(low_ref[pair].reshape(split).astype(F32) * grad_probs, axis=1, keepdims=True)
        gs_ref[pair] = (probs_ref[pair].reshape(split) * (grad_probs - delta)).astype(BF16).reshape(joined)

    def add_values(pair):
        gv[pair * kv_heads // pairs] += dot(low_ref[pair], g_ref[:, columns[pair]])

    def add_keys(pair):
        gk[pair * kv_heads // pairs] += dot(gs_ref[pair], q_ref[:, columns[pair]])

    def add_queries(pair):
        if early:
            copies.append(grad_queries_of(pair, gs_ref, k2[pair], gq_ref, gq_hbm, sems.at[pair]))

    for pair in range(pairs):
        score(pair)
        against_values(pair)
    for pair in range(pairs):
        soften(pair)
    for pair in range(pairs):
        grad_score(pair)
        add_values(pair)
    for pair in range(pairs):
        add_queries(pair)
    for pair in range(pairs):
        add_keys(pair)
    gk = [(part[:keys, :HEAD_DIM] + part[keys:, HEAD_DIM:]) * score_scale for part in gk]
    gv = [part[:keys, :HEAD_DIM] + part[keys:, HEAD_DIM:] for part in gv]
    terms = jnp.concatenate([jnp.concatenate(gk, 1), jnp.concatenate(gv, 1)], 0).astype(BF16)
    terms_ref[...] = dot(order, terms, 0, 0).astype(BF16)
    for copy in copies:
        copy.wait()


def attend_kernel(me_ref, *refs):
    pl.when(me_ref[0] == 0)(lambda: attend_body(True, *refs))
    pl.when(me_ref[0] != 0)(lambda: attend_body(False, *refs))


def sum_kernel(
    starts, me_ref, pick_ref, terms_ref, gs_ref, k_ref, log_ref, _, keys_hbm, values_hbm, log_hbm, gq_hbm,
    keys_ref, values_ref, gq_ref, sems
):
    per_owner, rows, _ = keys_ref.shape
    width = terms_ref.shape[1]
    done = {}
    for core, start in enumerate(starts):
        part = dot(pick_ref[core], terms_ref[...])
        done[start] = done[start] + part if start in done else part
    for start, total in done.items():
        for slot in range(per_owner):
            for place, ref in ((slot, keys_ref), (per_owner + slot, values_ref)):
                ref[slot, :, start : start + width] = total[place * rows : (place + 1) * rows].astype(BF16)
    pairs = gs_ref.shape[0]
    copies = [
        pltpu.make_async_copy(keys_ref, keys_hbm, sems.at[pairs]),
        pltpu.make_async_copy(values_ref, values_hbm, sems.at[pairs + 1]),
        pltpu.make_async_copy(log_ref, log_hbm, sems.at[pairs + 2]),
    ]
    for copy in copies:
        copy.start()

    @pl.when(me_ref[0] != 0)
    def _():
        kv_heads = k_ref.shape[1] // HEAD_DIM
        k2 = [block_diagonal(k_ref[:, kv * HEAD_DIM : (kv + 1) * HEAD_DIM]) for kv in range(kv_heads)]
        late = [
            grad_queries_of(pair, gs_ref, k2[pair * kv_heads // pairs], gq_ref, gq_hbm, sems.at[pair])
            for pair in range(pairs)
        ]
        for copy in late:
            copy.wait()

    for copy in copies:
        copy.wait()


def local(queries, keys, values, grad_out, block_map, block_count):
    spans, cores = lax.axis_size("seq"), lax.axis_size("vis")
    me = lax.axis_index("seq").astype(jnp.int32).reshape(1)
    per_owner, rows, _ = keys.shape
    tokens = queries.shape[0]
    heads = queries.shape[1] // HEAD_DIM
    most = block_map.shape[1]
    width = max(heads // GROUP, 1) * HEAD_DIM
    starts = tuple(core * heads // GROUP * HEAD_DIM for core in range(cores))
    attended = most * cores * rows
    travelling = cores * spans * 2 * rows
    order_of = exchange_order(spans, cores)
    places = jnp.asarray(np.repeat(np.divmod(np.array(order_of, np.int32), cores), 2 * rows, axis=1))
    shape = jax.ShapeDtypeStruct
    params = pltpu.CompilerParams(vmem_limit_bytes=24 * 1024 * 1024)
    stay = functools.partial(pltpu.with_memory_space_constraint, memory_space=pltpu.HBM)

    sent, pick, order, live = pl.pallas_call(
        functools.partial(choose_kernel, starts),
        out_shape=(
            shape((travelling, width), BF16),
            shape((cores, 2 * per_owner * rows, travelling), BF16),
            shape((2 * attended, travelling), BF16),
            shape((attended, tokens), F32),
        ),
        in_specs=[SMEM] + [HBM] * 5,
        out_specs=(VMEM,) * 4,
        scratch_shapes=[
            pltpu.VMEM((most, spans), jnp.int32),
            pltpu.VMEM((1, spans), jnp.int32),
            pltpu.VMEM(places.shape, jnp.int32),
            pltpu.VMEM(keys.shape, BF16),
            pltpu.VMEM(keys.shape, BF16),
            pltpu.SemaphoreType.DMA((5,)),
        ],
        compiler_params=params,
        cost_estimate=pl.CostEstimate(flops=10**10, bytes_accessed=10**6, transcendentals=0),
        name="choose_blocks",
    )(me, *map(stay, (block_map.T, block_count.reshape(1, spans), places, keys, values)))
    got = exchange(sent.reshape(cores * spans, 2 * rows, width), order_of)
    pair_shape = (heads // 2, 2 * attended, tokens)
    terms, grad_queries, logs, gs, k = pl.pallas_call(
        attend_kernel,
        out_shape=(
            shape((travelling, width), BF16),
            shape(queries.shape, BF16),
            shape((heads, tokens), F32),
            shape(pair_shape, BF16),
            shape((attended, width), BF16),
        ),
        in_specs=[SMEM] + [VMEM] * 5,
        out_specs=(VMEM, HBM, VMEM, VMEM, VMEM),
        scratch_shapes=[pltpu.VMEM(pair_shape, kind) for kind in (F32, F32, F32, BF16)]
        + [
            pltpu.VMEM(queries.shape, BF16),
            pltpu.SemaphoreType.DMA((heads // 2,)),
        ],
        compiler_params=params,
        name="attend",
    )(me, queries, grad_out, order, live, got.reshape(-1, width))
    back = exchange(terms.reshape(cores * spans, 2 * rows, width), order_of)
    grad_keys, grad_values, log_totals, grad_queries = pl.pallas_call(
        functools.partial(sum_kernel, starts),
        out_shape=(
            shape(keys.shape, BF16),
            shape(keys.shape, BF16),
            shape((heads, tokens), F32),
            shape(queries.shape, BF16),
        ),
        in_specs=[SMEM] + [VMEM] * 5 + [HBM],
        out_specs=(HBM,) * 4,
        scratch_shapes=[
            pltpu.VMEM(keys.shape, BF16),
            pltpu.VMEM(keys.shape, BF16),
            pltpu.VMEM(queries.shape, BF16),
            pltpu.SemaphoreType.DMA((heads // 2 + 3,)),
        ],
        input_output_aliases={6: 3},
        compiler_params=params,
        name="sum_blocks",
    )(me, pick, back.reshape(-1, width), gs, k, logs, grad_queries)
    return grad_queries, log_totals, grad_keys, grad_values


def solution(mesh):
    in_specs = (
        P("seq", "vis"),
        P("seq", "vis", None),
        P("seq", "vis", None),
        P("seq", "vis"),
        P(),
        P(),
    )
    out_specs = (P("seq", "vis"), P("vis", "seq"), P("seq", "vis", None), P("seq", "vis", None))
    return jax.shard_map(local, mesh=mesh, in_specs=in_specs, out_specs=out_specs, check_vma=False)
```

```python
import functools
import math

import jax
import jax.numpy as jnp
import numpy as np
from jax import lax
from jax.experimental import pallas as pl
from jax.experimental.pallas import tpu as pltpu
from jax.sharding import PartitionSpec as P

HEAD_DIM = 128
GROUP = 8
BF16 = jnp.bfloat16
F32 = jnp.float32
LOG2E = math.log2(math.e)
VMEM = pl.BlockSpec(memory_space=pltpu.VMEM)
HBM = pl.BlockSpec(memory_space=pltpu.HBM)
SMEM = pl.BlockSpec(memory_space=pltpu.SMEM)
EXCHANGE_ORDER = {
    (16, 2): [18, 27, 28, 3, 6, 21, 13, 15, 22, 4, 12, 30, 7, 16, 23, 14, 20, 9, 17, 10, 29, 11, 0, 19, 26, 2, 24, 5, 1, 8, 31, 25],
}


def exchange_order(spans, cores):
    return EXCHANGE_ORDER.get((spans, cores)) or [span * cores + core for core in range(cores) for span in range(spans)]


def exchange(parts, order):
    return lax.all_to_all(
        parts, ("seq", "vis"), split_axis=0, concat_axis=0, tiled=True, axis_index_groups=[list(order)]
    )


def iota(shape, dim):
    return lax.broadcasted_iota(jnp.int32, shape, dim)


def dot(left, right, left_dim=1, right_dim=0):
    return lax.dot_general(
        left, right, (((left_dim,), (right_dim,)), ((), ())), preferred_element_type=F32
    )


def load_kernel(*refs):
    sems, half = refs[-1], len(refs) // 2
    copies = [pltpu.make_async_copy(src, dst, sems.at[i]) for i, (src, dst) in enumerate(zip(refs[:half], refs[half:-1]))]
    for copy in copies:
        copy.start()
    for copy in copies:
        copy.wait()


def choose_kernel(
    starts, me_ref, map_ref, count_ref, place_ref, keys_ref, values_ref, out_ref, pick_ref, order_ref, live_ref
):
    me = me_ref[0]
    per_owner, rows, _ = keys_ref.shape
    most, spans = map_ref.shape
    cores = len(starts)

    _, slot_rows, travelling = pick_ref.shape
    width = out_ref.shape[1]
    have, part = iota((slot_rows, 1), 0), iota((1, travelling), 1) % (2 * rows)
    have_slot = (have % (per_owner * rows) // rows + 1).astype(F32)
    same_part = have // (per_owner * rows) * rows + have % rows == part

    block_rows = cores * rows
    keys = most * block_rows
    mine = iota((2 * keys, 1), 0)
    block = mine % keys // block_rows
    expand_blocks = (iota((2 * keys, most), 1) == block).astype(BF16)
    same_row = mine // keys * rows + mine % rows == part
    core = mine % block_rows // rows
    here = iota((1, spans), 1) == me
    live_block = iota(live_ref.shape, 0) // block_rows

    relative = map_ref[...] - me * per_owner
    asked = (relative >= 0) & (relative < per_owner) & (iota((most, spans), 0) < count_ref[...])
    slot = jnp.sum(jnp.where(asked, relative + 1, 0), axis=0, keepdims=True).astype(F32)
    place_span, place_core = place_ref[0:1, :], place_ref[1:2, :]
    lanes = 128
    slots = jnp.concatenate([slot, jnp.zeros((1, lanes - spans), F32)], axis=1)
    slots = jnp.broadcast_to(slots, (8, lanes))
    want = [
        jnp.take_along_axis(slots, jnp.broadcast_to(place_span[:, at : at + lanes], (8, lanes)), axis=1, mode="promise_in_bounds")[:1]
        for at in range(0, travelling, lanes)
    ]
    want = jnp.concatenate(want, axis=1)
    asked = (want == have_slot) & same_part
    stacked = [ref[slot].astype(F32) for ref in (keys_ref, values_ref) for slot in range(per_owner)]
    stacked = jnp.concatenate(stacked, axis=0).astype(BF16)
    out = 0.0
    for to, start in enumerate(starts):
        pick = (asked & (place_core == to)).astype(BF16)
        pick_ref[to] = pick
        out += dot(pick, stacked[:, start : start + width], 0, 0)
    out_ref[...] = out.astype(BF16)

    owners = jnp.sum(jnp.where(here, map_ref[...] // per_owner, 0), axis=1, keepdims=True)
    count = jnp.sum(jnp.where(here, count_ref[...], 0), axis=1, keepdims=True)
    lanes = jnp.broadcast_to(owners.astype(F32), (most, travelling)).astype(BF16)
    owner = dot(expand_blocks, lanes).astype(jnp.int32)
    order = same_row & (owner == place_span) & (core == place_core) & (block < count)
    order_ref[...] = order.astype(BF16)
    live_ref[...] = jnp.where(live_block < count, 0.0, -1e30)


def block_diagonal(part):
    zero = jnp.zeros_like(part)
    return jnp.concatenate([jnp.concatenate([part, zero], 1), jnp.concatenate([zero, part], 1)], 0)


def grad_queries_of(pair, gs_ref, k2, gq_ref, gq_hbm, sem):
    score_scale = 1.0 / math.sqrt(HEAD_DIM)
    at = slice(2 * pair * HEAD_DIM, 2 * (pair + 1) * HEAD_DIM)
    gq_ref[:, at] = (dot(gs_ref[pair], k2, 0, 0) * score_scale).astype(BF16)
    copy = pltpu.make_async_copy(gq_ref.at[:, at], gq_hbm.at[:, at], sem)
    copy.start()
    return copy


def attend_body(
    early, q_ref, g_ref, order_ref, live_ref, rows_ref, terms_ref, gq_hbm, log_ref, gs_ref, k_ref,
    scores_ref, gp_ref, probs_ref, low_ref, gq_ref, sems
):
    score_scale = 1.0 / math.sqrt(HEAD_DIM)
    keys, tokens = live_ref.shape
    kv_heads = rows_ref.shape[1] // HEAD_DIM
    pairs = gs_ref.shape[0]
    split, joined = (2, keys, tokens), (2 * keys, tokens)
    columns = [slice(2 * pair * HEAD_DIM, 2 * (pair + 1) * HEAD_DIM) for pair in range(pairs)]
    order, live = order_ref[...], live_ref[...]
    fetched = dot(order, rows_ref[...]).astype(BF16)
    k_ref[...] = fetched[:keys]
    heads = [fetched[:, kv * HEAD_DIM : (kv + 1) * HEAD_DIM] for kv in range(kv_heads)]
    k2 = [block_diagonal(head[:keys]) for head in heads for _ in range(pairs // kv_heads)]
    v2 = [block_diagonal(head[keys:]) for head in heads for _ in range(pairs // kv_heads)]

    copies = []
    gk, gv = [0.0] * kv_heads, [0.0] * kv_heads

    def score(pair):
        scores_ref[pair] = dot(k2[pair], q_ref[:, columns[pair]], 1, 1)

    def soften(pair):
        scores = scores_ref[pair].reshape(split) * (score_scale * LOG2E) + live
        row_max = jnp.max(scores, axis=1, keepdims=True)
        weights = jnp.exp2(scores - row_max)
        totals = jnp.sum(weights, axis=1, keepdims=True)
        probs = weights * (1.0 / totals)
        log_ref[2 * pair : 2 * pair + 2, :] = ((row_max + jnp.log2(totals)) * (1.0 / LOG2E)).reshape(2, tokens)
        probs_ref[pair] = probs.reshape(joined)
        low_ref[pair] = probs.astype(BF16).reshape(joined)

    def against_values(pair):
        gp_ref[pair] = dot(v2[pair], g_ref[:, columns[pair]], 1, 1)

    def grad_score(pair):
        grad_probs = gp_ref[pair].reshape(split)
        delta = jnp.sum(low_ref[pair].reshape(split).astype(F32) * grad_probs, axis=1, keepdims=True)
        gs_ref[pair] = (probs_ref[pair].reshape(split) * (grad_probs - delta)).astype(BF16).reshape(joined)

    def add_values(pair):
        gv[pair * kv_heads // pairs] += dot(low_ref[pair], g_ref[:, columns[pair]])

    def add_keys(pair):
        gk[pair * kv_heads // pairs] += dot(gs_ref[pair], q_ref[:, columns[pair]])

    def add_queries(pair):
        if early:
            copies.append(grad_queries_of(pair, gs_ref, k2[pair], gq_ref, gq_hbm, sems.at[pair]))

    for pair in range(pairs):
        score(pair)
        against_values(pair)
    for pair in range(pairs):
        soften(pair)
    for pair in range(pairs):
        grad_score(pair)
        add_values(pair)
    for pair in range(pairs):
        add_queries(pair)
    for pair in range(pairs):
        add_keys(pair)
    gk = [(part[:keys, :HEAD_DIM] + part[keys:, HEAD_DIM:]) * score_scale for part in gk]
    gv = [part[:keys, :HEAD_DIM] + part[keys:, HEAD_DIM:] for part in gv]
    terms = jnp.concatenate([jnp.concatenate(gk, 1), jnp.concatenate(gv, 1)], 0).astype(BF16)
    terms_ref[...] = dot(order, terms, 0, 0).astype(BF16)
    for copy in copies:
        copy.wait()


def attend_kernel(me_ref, *refs):
    pl.when(me_ref[0] == 0)(lambda: attend_body(True, *refs))
    pl.when(me_ref[0] != 0)(lambda: attend_body(False, *refs))


def sum_kernel(
    starts, me_ref, pick_ref, terms_ref, gs_ref, k_ref, log_ref, _, keys_hbm, values_hbm, log_hbm, gq_hbm,
    keys_ref, values_ref, gq_ref, sems
):
    per_owner, rows, _ = keys_ref.shape
    width = terms_ref.shape[1]
    done = {}
    for core, start in enumerate(starts):
        part = dot(pick_ref[core], terms_ref[...])
        done[start] = done[start] + part if start in done else part
    for start, total in done.items():
        for slot in range(per_owner):
            for place, ref in ((slot, keys_ref), (per_owner + slot, values_ref)):
                ref[slot, :, start : start + width] = total[place * rows : (place + 1) * rows].astype(BF16)
    pairs = gs_ref.shape[0]
    copies = [
        pltpu.make_async_copy(keys_ref, keys_hbm, sems.at[pairs]),
        pltpu.make_async_copy(values_ref, values_hbm, sems.at[pairs + 1]),
        pltpu.make_async_copy(log_ref, log_hbm, sems.at[pairs + 2]),
    ]
    for copy in copies:
        copy.start()

    @pl.when(me_ref[0] != 0)
    def _():
        kv_heads = k_ref.shape[1] // HEAD_DIM
        k2 = [block_diagonal(k_ref[:, kv * HEAD_DIM : (kv + 1) * HEAD_DIM]) for kv in range(kv_heads)]
        late = [
            grad_queries_of(pair, gs_ref, k2[pair * kv_heads // pairs], gq_ref, gq_hbm, sems.at[pair])
            for pair in range(pairs)
        ]
        for copy in late:
            copy.wait()

    for copy in copies:
        copy.wait()


def local(queries, keys, values, grad_out, block_map, block_count):
    spans, cores = lax.axis_size("seq"), lax.axis_size("vis")
    me = lax.axis_index("seq").astype(jnp.int32).reshape(1)
    per_owner, rows, _ = keys.shape
    tokens = queries.shape[0]
    heads = queries.shape[1] // HEAD_DIM
    most = block_map.shape[1]
    width = max(heads // GROUP, 1) * HEAD_DIM
    starts = tuple(core * heads // GROUP * HEAD_DIM for core in range(cores))
    attended = most * cores * rows
    travelling = cores * spans * 2 * rows
    order_of = exchange_order(spans, cores)
    places = jnp.asarray(np.repeat(np.divmod(np.array(order_of, np.int32), cores), 2 * rows, axis=1))
    shape = jax.ShapeDtypeStruct
    params = pltpu.CompilerParams(vmem_limit_bytes=24 * 1024 * 1024)
    stay = functools.partial(pltpu.with_memory_space_constraint, memory_space=pltpu.HBM)

    inputs = (block_map.T, block_count.reshape(1, spans), places, keys, values)
    inputs = pl.pallas_call(
        load_kernel,
        out_shape=tuple(shape(part.shape, part.dtype) for part in inputs),
        in_specs=[HBM] * 5,
        out_specs=(VMEM,) * 5,
        scratch_shapes=[pltpu.SemaphoreType.DMA((5,))],
        compiler_params=params,
        name="load_blocks",
    )(*map(stay, inputs))
    sent, pick, order, live = pl.pallas_call(
        functools.partial(choose_kernel, starts),
        out_shape=(
            shape((travelling, width), BF16),
            shape((cores, 2 * per_owner * rows, travelling), BF16),
            shape((2 * attended, travelling), BF16),
            shape((attended, tokens), F32),
        ),
        in_specs=[SMEM] + [VMEM] * 5,
        out_specs=(VMEM,) * 4,
        compiler_params=params,
        cost_estimate=pl.CostEstimate(flops=10**10, bytes_accessed=10**6, transcendentals=0),
        name="choose_blocks",
    )(me, *inputs)
    got = exchange(sent.reshape(cores * spans, 2 * rows, width), order_of)
    pair_shape = (heads // 2, 2 * attended, tokens)
    terms, grad_queries, logs, gs, k = pl.pallas_call(
        attend_kernel,
        out_shape=(
            shape((travelling, width), BF16),
            shape(queries.shape, BF16),
            shape((heads, tokens), F32),
            shape(pair_shape, BF16),
            shape((attended, width), BF16),
        ),
        in_specs=[SMEM] + [VMEM] * 5,
        out_specs=(VMEM, HBM, VMEM, VMEM, VMEM),
        scratch_shapes=[pltpu.VMEM(pair_shape, kind) for kind in (F32, F32, F32, BF16)]
        + [
            pltpu.VMEM(queries.shape, BF16),
            pltpu.SemaphoreType.DMA((heads // 2,)),
        ],
        compiler_params=params,
        name="attend",
    )(me, queries, grad_out, order, live, got.reshape(-1, width))
    back = exchange(terms.reshape(cores * spans, 2 * rows, width), order_of)
    grad_keys, grad_values, log_totals, grad_queries = pl.pallas_call(
        functools.partial(sum_kernel, starts),
        out_shape=(
            shape(keys.shape, BF16),
            shape(keys.shape, BF16),
            shape((heads, tokens), F32),
            shape(queries.shape, BF16),
        ),
        in_specs=[SMEM] + [VMEM] * 5 + [HBM],
        out_specs=(HBM,) * 4,
        scratch_shapes=[
            pltpu.VMEM(keys.shape, BF16),
            pltpu.VMEM(keys.shape, BF16),
            pltpu.VMEM(queries.shape, BF16),
            pltpu.SemaphoreType.DMA((heads // 2 + 3,)),
        ],
        input_output_aliases={6: 3},
        compiler_params=params,
        name="sum_blocks",
    )(me, pick, back.reshape(-1, width), gs, k, logs, grad_queries)
    return grad_queries, log_totals, grad_keys, grad_values


def solution(mesh):
    in_specs = (
        P("seq", "vis"),
        P("seq", "vis", None),
        P("seq", "vis", None),
        P("seq", "vis"),
        P(),
        P(),
    )
    out_specs = (P("seq", "vis"), P("vis", "seq"), P("seq", "vis", None), P("seq", "vis", None))
    return jax.shard_map(local, mesh=mesh, in_specs=in_specs, out_specs=out_specs, check_vma=False)
```

```python
import functools
import math

import jax
import jax.numpy as jnp
import numpy as np
from jax import lax
from jax.experimental import pallas as pl
from jax.experimental.pallas import tpu as pltpu
from jax.sharding import PartitionSpec as P

HEAD_DIM = 128
GROUP = 8
BF16 = jnp.bfloat16
F32 = jnp.float32
LOG2E = math.log2(math.e)
VMEM = pl.BlockSpec(memory_space=pltpu.VMEM)
HBM = pl.BlockSpec(memory_space=pltpu.HBM)
SMEM = pl.BlockSpec(memory_space=pltpu.SMEM)
EXCHANGE_ORDER = {
    (16, 2): [18, 27, 28, 3, 6, 21, 13, 15, 22, 4, 12, 30, 7, 16, 23, 14, 20, 9, 17, 10, 29, 11, 0, 19, 26, 2, 24, 5, 1, 8, 31, 25],
}


def exchange_order(spans, cores):
    return EXCHANGE_ORDER.get((spans, cores)) or [span * cores + core for core in range(cores) for span in range(spans)]


def exchange(parts, order):
    return lax.all_to_all(
        parts, ("seq", "vis"), split_axis=0, concat_axis=0, tiled=True, axis_index_groups=[list(order)]
    )


def iota(shape, dim):
    return lax.broadcasted_iota(jnp.int32, shape, dim)


def dot(left, right, left_dim=1, right_dim=0):
    return lax.dot_general(
        left, right, (((left_dim,), (right_dim,)), ((), ())), preferred_element_type=F32
    )


def load_kernel(*refs):
    sems, half = refs[-1], len(refs) // 2
    copies = [pltpu.make_async_copy(src, dst, sems.at[i]) for i, (src, dst) in enumerate(zip(refs[:half], refs[half:-1]))]
    for copy in copies:
        copy.start()
    for copy in copies:
        copy.wait()


def choose_kernel(
    starts, me_ref, map_ref, count_ref, place_ref, keys_ref, values_ref, out_ref, pick_ref, order_ref, live_ref
):
    me = me_ref[0]
    per_owner, rows, _ = keys_ref.shape
    most, spans = map_ref.shape
    cores = len(starts)

    pick_rows, travelling = pick_ref.shape
    slot_rows = pick_rows // cores
    width = out_ref.shape[1]
    place_span, place_core = place_ref[0:1, :], place_ref[1:2, :]
    have, part = iota((pick_rows, 1), 0), iota((1, travelling), 1) % (2 * rows)
    have_slot = (have % (per_owner * rows) // rows + 1).astype(F32)
    same_part = have % slot_rows // (per_owner * rows) * rows + have % rows == part
    same_place = same_part & (have // slot_rows == place_core)

    block_rows = cores * rows
    keys = most * block_rows
    mine = iota((2 * keys, 1), 0)
    block = mine % keys // block_rows
    expand_blocks = (iota((2 * keys, most), 1) == block).astype(BF16)
    same_row = mine // keys * rows + mine % rows == part
    core = mine % block_rows // rows
    here = iota((1, spans), 1) == me
    live_block = iota(live_ref.shape, 0) // block_rows

    relative = map_ref[...] - me * per_owner
    asked = (relative >= 0) & (relative < per_owner) & (iota((most, spans), 0) < count_ref[...])
    slot = jnp.sum(jnp.where(asked, relative + 1, 0), axis=0, keepdims=True).astype(F32)
    lanes = 128
    slots = jnp.concatenate([slot, jnp.zeros((1, lanes - spans), F32)], axis=1)
    slots = jnp.broadcast_to(slots, (8, lanes))
    want = [
        jnp.take_along_axis(slots, jnp.broadcast_to(place_span[:, at : at + lanes], (8, lanes)), axis=1, mode="promise_in_bounds")[:1]
        for at in range(0, travelling, lanes)
    ]
    want = jnp.concatenate(want, axis=1)
    pick = ((want == have_slot) & same_place).astype(BF16)
    pick_ref[...] = pick
    stacked = [ref[slot].astype(F32) for ref in (keys_ref, values_ref) for slot in range(per_owner)]
    stacked = jnp.concatenate(stacked, axis=0).astype(BF16)
    stacked = jnp.concatenate([stacked[:, start : start + width] for start in starts], axis=0)
    out_ref[...] = dot(pick, stacked, 0, 0).astype(BF16)

    owners = jnp.sum(jnp.where(here, map_ref[...] // per_owner, 0), axis=1, keepdims=True)
    count = jnp.sum(jnp.where(here, count_ref[...], 0), axis=1, keepdims=True)
    lanes = jnp.broadcast_to(owners.astype(F32), (most, travelling)).astype(BF16)
    owner = dot(expand_blocks, lanes).astype(jnp.int32)
    order = same_row & (owner == place_span) & (core == place_core) & (block < count)
    order_ref[...] = order.astype(BF16)
    live_ref[...] = jnp.where(live_block < count, 0.0, -1e30)


def block_diagonal(part):
    zero = jnp.zeros_like(part)
    return jnp.concatenate([jnp.concatenate([part, zero], 1), jnp.concatenate([zero, part], 1)], 0)


def grad_queries_of(pair, gs_ref, k2, gq_ref, gq_hbm, sem):
    score_scale = 1.0 / math.sqrt(HEAD_DIM)
    at = slice(2 * pair * HEAD_DIM, 2 * (pair + 1) * HEAD_DIM)
    gq_ref[:, at] = (dot(gs_ref[pair], k2, 0, 0) * score_scale).astype(BF16)
    copy = pltpu.make_async_copy(gq_ref.at[:, at], gq_hbm.at[:, at], sem)
    copy.start()
    return copy


def attend_body(
    early, q_ref, g_ref, order_ref, live_ref, rows_ref, terms_ref, gq_hbm, log_ref, gs_ref, k_ref,
    scores_ref, gp_ref, probs_ref, low_ref, gq_ref, sems
):
    score_scale = 1.0 / math.sqrt(HEAD_DIM)
    keys, tokens = live_ref.shape
    kv_heads = rows_ref.shape[1] // HEAD_DIM
    pairs = gs_ref.shape[0]
    split, joined = (2, keys, tokens), (2 * keys, tokens)
    columns = [slice(2 * pair * HEAD_DIM, 2 * (pair + 1) * HEAD_DIM) for pair in range(pairs)]
    order, live = order_ref[...], live_ref[...]
    fetched = dot(order, rows_ref[...]).astype(BF16)
    k_ref[...] = fetched[:keys]
    heads = [fetched[:, kv * HEAD_DIM : (kv + 1) * HEAD_DIM] for kv in range(kv_heads)]
    k2 = [block_diagonal(head[:keys]) for head in heads for _ in range(pairs // kv_heads)]
    v2 = [block_diagonal(head[keys:]) for head in heads for _ in range(pairs // kv_heads)]

    copies = []
    gk, gv = [0.0] * kv_heads, [0.0] * kv_heads

    def score(pair):
        scores_ref[pair] = dot(k2[pair], q_ref[:, columns[pair]], 1, 1)

    def soften(pair):
        scores = scores_ref[pair].reshape(split) * (score_scale * LOG2E) + live
        row_max = jnp.max(scores, axis=1, keepdims=True)
        weights = jnp.exp2(scores - row_max)
        totals = jnp.sum(weights, axis=1, keepdims=True)
        probs = weights * (1.0 / totals)
        log_ref[2 * pair : 2 * pair + 2, :] = ((row_max + jnp.log2(totals)) * (1.0 / LOG2E)).reshape(2, tokens)
        probs_ref[pair] = probs.reshape(joined)
        low_ref[pair] = probs.astype(BF16).reshape(joined)

    def against_values(pair):
        gp_ref[pair] = dot(v2[pair], g_ref[:, columns[pair]], 1, 1)

    def grad_score(pair):
        grad_probs = gp_ref[pair].reshape(split)
        delta = jnp.sum(low_ref[pair].reshape(split).astype(F32) * grad_probs, axis=1, keepdims=True)
        gs_ref[pair] = (probs_ref[pair].reshape(split) * (grad_probs - delta)).astype(BF16).reshape(joined)

    def add_values(pair):
        gv[pair * kv_heads // pairs] += dot(low_ref[pair], g_ref[:, columns[pair]])

    def add_keys(pair):
        gk[pair * kv_heads // pairs] += dot(gs_ref[pair], q_ref[:, columns[pair]])

    def add_queries(pair):
        if early:
            copies.append(grad_queries_of(pair, gs_ref, k2[pair], gq_ref, gq_hbm, sems.at[pair]))

    for pair in range(pairs):
        score(pair)
        against_values(pair)
    for pair in range(pairs):
        soften(pair)
    for pair in range(pairs):
        grad_score(pair)
        add_values(pair)
    for pair in range(pairs):
        add_queries(pair)
    for pair in range(pairs):
        add_keys(pair)
    gk = [(part[:keys, :HEAD_DIM] + part[keys:, HEAD_DIM:]) * score_scale for part in gk]
    gv = [part[:keys, :HEAD_DIM] + part[keys:, HEAD_DIM:] for part in gv]
    terms = jnp.concatenate([jnp.concatenate(gk, 1), jnp.concatenate(gv, 1)], 0).astype(BF16)
    terms_ref[...] = dot(order, terms, 0, 0).astype(BF16)
    for copy in copies:
        copy.wait()


def attend_kernel(me_ref, *refs):
    pl.when(me_ref[0] == 0)(lambda: attend_body(True, *refs))
    pl.when(me_ref[0] != 0)(lambda: attend_body(False, *refs))


def sum_kernel(
    starts, me_ref, pick_ref, terms_ref, gs_ref, k_ref, log_ref, _, keys_hbm, values_hbm, log_hbm, gq_hbm,
    keys_ref, values_ref, gq_ref, sems
):
    per_owner, rows, _ = keys_ref.shape
    width = terms_ref.shape[1]
    totals = dot(pick_ref[...], terms_ref[...])
    slot_rows = 2 * per_owner * rows
    done = {}
    for core, start in enumerate(starts):
        part = totals[core * slot_rows : (core + 1) * slot_rows]
        done[start] = done[start] + part if start in done else part
    for start, total in done.items():
        for slot in range(per_owner):
            for place, ref in ((slot, keys_ref), (per_owner + slot, values_ref)):
                ref[slot, :, start : start + width] = total[place * rows : (place + 1) * rows].astype(BF16)
    pairs = gs_ref.shape[0]
    copies = [
        pltpu.make_async_copy(keys_ref, keys_hbm, sems.at[pairs]),
        pltpu.make_async_copy(values_ref, values_hbm, sems.at[pairs + 1]),
        pltpu.make_async_copy(log_ref, log_hbm, sems.at[pairs + 2]),
    ]
    for copy in copies:
        copy.start()

    @pl.when(me_ref[0] != 0)
    def _():
        kv_heads = k_ref.shape[1] // HEAD_DIM
        k2 = [block_diagonal(k_ref[:, kv * HEAD_DIM : (kv + 1) * HEAD_DIM]) for kv in range(kv_heads)]
        late = [
            grad_queries_of(pair, gs_ref, k2[pair * kv_heads // pairs], gq_ref, gq_hbm, sems.at[pair])
            for pair in range(pairs)
        ]
        for copy in late:
            copy.wait()

    for copy in copies:
        copy.wait()


def local(queries, keys, values, grad_out, block_map, block_count):
    spans, cores = lax.axis_size("seq"), lax.axis_size("vis")
    me = lax.axis_index("seq").astype(jnp.int32).reshape(1)
    per_owner, rows, _ = keys.shape
    tokens = queries.shape[0]
    heads = queries.shape[1] // HEAD_DIM
    most = block_map.shape[1]
    width = max(heads // GROUP, 1) * HEAD_DIM
    starts = tuple(core * heads // GROUP * HEAD_DIM for core in range(cores))
    attended = most * cores * rows
    travelling = cores * spans * 2 * rows
    order_of = exchange_order(spans, cores)
    places = jnp.asarray(np.repeat(np.divmod(np.array(order_of, np.int32), cores), 2 * rows, axis=1))
    shape = jax.ShapeDtypeStruct
    params = pltpu.CompilerParams(vmem_limit_bytes=24 * 1024 * 1024)
    stay = functools.partial(pltpu.with_memory_space_constraint, memory_space=pltpu.HBM)

    inputs = (block_map.T, block_count.reshape(1, spans), places, keys, values)
    inputs = pl.pallas_call(
        load_kernel,
        out_shape=tuple(shape(part.shape, part.dtype) for part in inputs),
        in_specs=[HBM] * 5,
        out_specs=(VMEM,) * 5,
        scratch_shapes=[pltpu.SemaphoreType.DMA((5,))],
        compiler_params=params,
        name="load_blocks",
    )(*map(stay, inputs))
    sent, pick, order, live = pl.pallas_call(
        functools.partial(choose_kernel, starts),
        out_shape=(
            shape((travelling, width), BF16),
            shape((cores * 2 * per_owner * rows, travelling), BF16),
            shape((2 * attended, travelling), BF16),
            shape((attended, tokens), F32),
        ),
        in_specs=[SMEM] + [VMEM] * 5,
        out_specs=(VMEM,) * 4,
        compiler_params=params,
        cost_estimate=pl.CostEstimate(flops=10**10, bytes_accessed=10**6, transcendentals=0),
        name="choose_blocks",
    )(me, *inputs)
    got = exchange(sent.reshape(cores * spans, 2 * rows, width), order_of)
    pair_shape = (heads // 2, 2 * attended, tokens)
    terms, grad_queries, logs, gs, k = pl.pallas_call(
        attend_kernel,
        out_shape=(
            shape((travelling, width), BF16),
            shape(queries.shape, BF16),
            shape((heads, tokens), F32),
            shape(pair_shape, BF16),
            shape((attended, width), BF16),
        ),
        in_specs=[SMEM] + [VMEM] * 5,
        out_specs=(VMEM, HBM, VMEM, VMEM, VMEM),
        scratch_shapes=[pltpu.VMEM(pair_shape, kind) for kind in (F32, F32, F32, BF16)]
        + [
            pltpu.VMEM(queries.shape, BF16),
            pltpu.SemaphoreType.DMA((heads // 2,)),
        ],
        compiler_params=params,
        name="attend",
    )(me, queries, grad_out, order, live, got.reshape(-1, width))
    back = exchange(terms.reshape(cores * spans, 2 * rows, width), order_of)
    grad_keys, grad_values, log_totals, grad_queries = pl.pallas_call(
        functools.partial(sum_kernel, starts),
        out_shape=(
            shape(keys.shape, BF16),
            shape(keys.shape, BF16),
            shape((heads, tokens), F32),
            shape(queries.shape, BF16),
        ),
        in_specs=[SMEM] + [VMEM] * 5 + [HBM],
        out_specs=(HBM,) * 4,
        scratch_shapes=[
            pltpu.VMEM(keys.shape, BF16),
            pltpu.VMEM(keys.shape, BF16),
            pltpu.VMEM(queries.shape, BF16),
            pltpu.SemaphoreType.DMA((heads // 2 + 3,)),
        ],
        input_output_aliases={6: 3},
        compiler_params=params,
        name="sum_blocks",
    )(me, pick, back.reshape(-1, width), gs, k, logs, grad_queries)
    return grad_queries, log_totals, grad_keys, grad_values


def solution(mesh):
    in_specs = (
        P("seq", "vis"),
        P("seq", "vis", None),
        P("seq", "vis", None),
        P("seq", "vis"),
        P(),
        P(),
    )
    out_specs = (P("seq", "vis"), P("vis", "seq"), P("seq", "vis", None), P("seq", "vis", None))
    return jax.shard_map(local, mesh=mesh, in_specs=in_specs, out_specs=out_specs, check_vma=False)
```

```python
import functools
import math

import jax
import jax.numpy as jnp
import numpy as np
from jax import lax
from jax.experimental import pallas as pl
from jax.experimental.pallas import tpu as pltpu
from jax.sharding import PartitionSpec as P

HEAD_DIM = 128
GROUP = 8
BF16 = jnp.bfloat16
F32 = jnp.float32
LOG2E = math.log2(math.e)
VMEM = pl.BlockSpec(memory_space=pltpu.VMEM)
HBM = pl.BlockSpec(memory_space=pltpu.HBM)
SMEM = pl.BlockSpec(memory_space=pltpu.SMEM)
EXCHANGE_ORDER = {
    (16, 2): [18, 27, 28, 3, 6, 21, 13, 15, 22, 4, 12, 30, 7, 16, 23, 14, 20, 9, 17, 10, 29, 11, 0, 19, 26, 2, 24, 5, 1, 8, 31, 25],
}


def exchange_order(spans, cores):
    return EXCHANGE_ORDER.get((spans, cores)) or [span * cores + core for core in range(cores) for span in range(spans)]


def exchange(parts, order):
    return lax.all_to_all(
        parts, ("seq", "vis"), split_axis=0, concat_axis=0, tiled=True, axis_index_groups=[list(order)]
    )


def iota(shape, dim):
    return lax.broadcasted_iota(jnp.int32, shape, dim)


def dot(left, right, left_dim=1, right_dim=0):
    return lax.dot_general(
        left, right, (((left_dim,), (right_dim,)), ((), ())), preferred_element_type=F32
    )


def load_kernel(*refs):
    sems, half = refs[-1], len(refs) // 2
    copies = [pltpu.make_async_copy(src, dst, sems.at[i]) for i, (src, dst) in enumerate(zip(refs[:half], refs[half:-1]))]
    for copy in copies:
        copy.start()
    for copy in copies:
        copy.wait()


def choose_kernel(
    starts, me_ref, map_ref, count_ref, place_ref, keys_ref, values_ref, out_ref, pick_ref, order_ref, live_ref
):
    me = me_ref[0]
    per_owner, rows, _ = keys_ref.shape
    most, spans = map_ref.shape
    cores = len(starts)

    pick_rows, travelling = pick_ref.shape
    slot_rows = pick_rows // cores
    width = out_ref.shape[1]
    place_span, place_core = place_ref[0:1, :], place_ref[1:2, :]
    have, part = iota((pick_rows, 1), 0), iota((1, travelling), 1) % (2 * rows)
    have_slot = (have % (per_owner * rows) // rows + 1).astype(F32)
    same_part = have % slot_rows // (per_owner * rows) * rows + have % rows == part
    same_place = same_part & (have // slot_rows == place_core)

    block_rows = cores * rows
    keys = most * block_rows
    mine = iota((2 * keys, 1), 0)
    block = mine % keys // block_rows
    expand_blocks = (iota((2 * keys, most), 1) == block).astype(BF16)
    same_row = mine // keys * rows + mine % rows == part
    core = mine % block_rows // rows
    here = iota((1, spans), 1) == me
    live_block = iota(live_ref.shape, 0) // block_rows

    relative = map_ref[...] - me * per_owner
    asked = (relative >= 0) & (relative < per_owner) & (iota((most, spans), 0) < count_ref[...])
    slot = jnp.sum(jnp.where(asked, relative + 1, 0), axis=0, keepdims=True).astype(F32)
    lanes = 128
    slots = jnp.concatenate([slot, jnp.zeros((1, lanes - spans), F32)], axis=1)
    slots = jnp.broadcast_to(slots, (8, lanes))
    want = [
        jnp.take_along_axis(slots, jnp.broadcast_to(place_span[:, at : at + lanes], (8, lanes)), axis=1, mode="promise_in_bounds")[:1]
        for at in range(0, travelling, lanes)
    ]
    want = jnp.concatenate(want, axis=1)
    pick = ((want == have_slot) & same_place).astype(BF16)
    pick_ref[...] = pick
    stacked = [ref[slot].astype(F32) for ref in (keys_ref, values_ref) for slot in range(per_owner)]
    stacked = jnp.concatenate(stacked, axis=0).astype(BF16)
    stacked = jnp.concatenate([stacked[:, start : start + width] for start in starts], axis=0)
    out_ref[...] = dot(pick, stacked, 0, 0).astype(BF16)

    owners = jnp.sum(jnp.where(here, map_ref[...] // per_owner, 0), axis=1, keepdims=True)
    count = jnp.sum(jnp.where(here, count_ref[...], 0), axis=1, keepdims=True)
    lanes = jnp.broadcast_to(owners.astype(F32), (most, travelling)).astype(BF16)
    owner = dot(expand_blocks, lanes).astype(jnp.int32)
    order = same_row & (owner == place_span) & (core == place_core) & (block < count)
    order_ref[...] = order.astype(BF16)
    live_ref[...] = jnp.where(live_block < count, 0.0, -1e30)


def block_diagonal(part):
    zero = jnp.zeros_like(part)
    return jnp.concatenate([jnp.concatenate([part, zero], 1), jnp.concatenate([zero, part], 1)], 0)


def grad_queries_of(pair, gs_ref, k2, gq_ref, gq_hbm, sem):
    score_scale = 1.0 / math.sqrt(HEAD_DIM)
    at = slice(2 * pair * HEAD_DIM, 2 * (pair + 1) * HEAD_DIM)
    gq_ref[:, at] = (dot(gs_ref[pair], k2, 0, 0) * score_scale).astype(BF16)
    copy = pltpu.make_async_copy(gq_ref.at[:, at], gq_hbm.at[:, at], sem)
    copy.start()
    return copy


def attend_body(
    early, q_ref, g_ref, order_ref, live_ref, rows_ref, terms_ref, gq_hbm, log_ref, gs_ref, k_ref,
    scores_ref, gp_ref, probs_ref, low_ref, gq_ref, sems
):
    score_scale = 1.0 / math.sqrt(HEAD_DIM)
    keys, tokens = live_ref.shape
    kv_heads = rows_ref.shape[1] // HEAD_DIM
    pairs = gs_ref.shape[0]
    split, joined = (2, keys, tokens), (2 * keys, tokens)
    columns = [slice(2 * pair * HEAD_DIM, 2 * (pair + 1) * HEAD_DIM) for pair in range(pairs)]
    order, live = order_ref[...], live_ref[...]
    fetched = dot(order, rows_ref[...]).astype(BF16)
    k_ref[...] = fetched[:keys]
    heads = [fetched[:, kv * HEAD_DIM : (kv + 1) * HEAD_DIM] for kv in range(kv_heads)]
    k2 = [block_diagonal(head[:keys]) for head in heads for _ in range(pairs // kv_heads)]
    v2 = [block_diagonal(head[keys:]) for head in heads for _ in range(pairs // kv_heads)]

    copies = []
    gk, gv = [0.0] * kv_heads, [0.0] * kv_heads

    def score(pair):
        scores_ref[pair] = dot(k2[pair], q_ref[:, columns[pair]], 1, 1)

    def soften(pair):
        scores = scores_ref[pair].reshape(split) * (score_scale * LOG2E) + live
        row_max = jnp.max(scores, axis=1, keepdims=True)
        weights = jnp.exp2(scores - row_max)
        totals = jnp.sum(weights, axis=1, keepdims=True)
        probs = weights * (1.0 / totals)
        log_ref[2 * pair : 2 * pair + 2, :] = ((row_max + jnp.log2(totals)) * (1.0 / LOG2E)).reshape(2, tokens)
        probs_ref[pair] = probs.reshape(joined)
        low_ref[pair] = probs.astype(BF16).reshape(joined)

    def against_values(pair):
        gp_ref[pair] = dot(v2[pair], g_ref[:, columns[pair]], 1, 1)

    def grad_score(pair):
        grad_probs = gp_ref[pair].reshape(split)
        delta = jnp.sum(low_ref[pair].reshape(split).astype(F32) * grad_probs, axis=1, keepdims=True)
        gs_ref[pair] = (probs_ref[pair].reshape(split) * (grad_probs - delta)).astype(BF16).reshape(joined)

    def add_values(pair):
        gv[pair * kv_heads // pairs] += dot(low_ref[pair], g_ref[:, columns[pair]])

    def add_keys(pair):
        gk[pair * kv_heads // pairs] += dot(gs_ref[pair], q_ref[:, columns[pair]])

    def add_queries(pair):
        if early:
            copies.append(grad_queries_of(pair, gs_ref, k2[pair], gq_ref, gq_hbm, sems.at[pair]))

    for pair in range(pairs):
        score(pair)
        against_values(pair)
    for pair in range(pairs):
        soften(pair)
        add_values(pair)
    for pair in range(pairs):
        grad_score(pair)
    for pair in range(pairs):
        add_queries(pair)
    for pair in range(pairs):
        add_keys(pair)
    gk = [(part[:keys, :HEAD_DIM] + part[keys:, HEAD_DIM:]) * score_scale for part in gk]
    gv = [part[:keys, :HEAD_DIM] + part[keys:, HEAD_DIM:] for part in gv]
    terms = jnp.concatenate([jnp.concatenate(gk, 1), jnp.concatenate(gv, 1)], 0).astype(BF16)
    terms_ref[...] = dot(order, terms, 0, 0).astype(BF16)
    for copy in copies:
        copy.wait()


def attend_kernel(me_ref, *refs):
    pl.when(me_ref[0] == 0)(lambda: attend_body(True, *refs))
    pl.when(me_ref[0] != 0)(lambda: attend_body(False, *refs))


def sum_kernel(
    starts, me_ref, pick_ref, terms_ref, gs_ref, k_ref, log_ref, _, keys_hbm, values_hbm, log_hbm, gq_hbm,
    keys_ref, values_ref, gq_ref, sems
):
    per_owner, rows, _ = keys_ref.shape
    width = terms_ref.shape[1]
    totals = dot(pick_ref[...], terms_ref[...])
    slot_rows = 2 * per_owner * rows
    done = {}
    for core, start in enumerate(starts):
        part = totals[core * slot_rows : (core + 1) * slot_rows]
        done[start] = done[start] + part if start in done else part
    for start, total in done.items():
        for slot in range(per_owner):
            for place, ref in ((slot, keys_ref), (per_owner + slot, values_ref)):
                ref[slot, :, start : start + width] = total[place * rows : (place + 1) * rows].astype(BF16)
    pairs = gs_ref.shape[0]
    copies = [
        pltpu.make_async_copy(keys_ref, keys_hbm, sems.at[pairs]),
        pltpu.make_async_copy(values_ref, values_hbm, sems.at[pairs + 1]),
        pltpu.make_async_copy(log_ref, log_hbm, sems.at[pairs + 2]),
    ]
    for copy in copies:
        copy.start()

    @pl.when(me_ref[0] != 0)
    def _():
        kv_heads = k_ref.shape[1] // HEAD_DIM
        k2 = [block_diagonal(k_ref[:, kv * HEAD_DIM : (kv + 1) * HEAD_DIM]) for kv in range(kv_heads)]
        late = [
            grad_queries_of(pair, gs_ref, k2[pair * kv_heads // pairs], gq_ref, gq_hbm, sems.at[pair])
            for pair in range(pairs)
        ]
        for copy in late:
            copy.wait()

    for copy in copies:
        copy.wait()


def local(queries, keys, values, grad_out, block_map, block_count):
    spans, cores = lax.axis_size("seq"), lax.axis_size("vis")
    me = lax.axis_index("seq").astype(jnp.int32).reshape(1)
    per_owner, rows, _ = keys.shape
    tokens = queries.shape[0]
    heads = queries.shape[1] // HEAD_DIM
    most = block_map.shape[1]
    width = max(heads // GROUP, 1) * HEAD_DIM
    starts = tuple(core * heads // GROUP * HEAD_DIM for core in range(cores))
    attended = most * cores * rows
    travelling = cores * spans * 2 * rows
    order_of = exchange_order(spans, cores)
    places = jnp.asarray(np.repeat(np.divmod(np.array(order_of, np.int32), cores), 2 * rows, axis=1))
    shape = jax.ShapeDtypeStruct
    params = pltpu.CompilerParams(vmem_limit_bytes=24 * 1024 * 1024)
    stay = functools.partial(pltpu.with_memory_space_constraint, memory_space=pltpu.HBM)

    inputs = (block_map.T, block_count.reshape(1, spans), places)
    inputs = pl.pallas_call(
        load_kernel,
        out_shape=tuple(shape(part.shape, part.dtype) for part in inputs),
        in_specs=[HBM] * 3,
        out_specs=(VMEM,) * 3,
        scratch_shapes=[pltpu.SemaphoreType.DMA((3,))],
        compiler_params=params,
        cost_estimate=pl.CostEstimate(flops=10**9, bytes_accessed=10**6, transcendentals=0),
        name="load_blocks",
    )(*map(stay, inputs))
    sent, pick, order, live = pl.pallas_call(
        functools.partial(choose_kernel, starts),
        out_shape=(
            shape((travelling, width), BF16),
            shape((cores * 2 * per_owner * rows, travelling), BF16),
            shape((2 * attended, travelling), BF16),
            shape((attended, tokens), F32),
        ),
        in_specs=[SMEM] + [VMEM] * 5,
        out_specs=(VMEM,) * 4,
        compiler_params=params,
        cost_estimate=pl.CostEstimate(flops=10**10, bytes_accessed=10**6, transcendentals=0),
        name="choose_blocks",
    )(me, *inputs, keys, values)
    got = exchange(sent.reshape(cores * spans, 2 * rows, width), order_of)
    pair_shape = (heads // 2, 2 * attended, tokens)
    terms, grad_queries, logs, gs, k = pl.pallas_call(
        attend_kernel,
        out_shape=(
            shape((travelling, width), BF16),
            shape(queries.shape, BF16),
            shape((heads, tokens), F32),
            shape(pair_shape, BF16),
            shape((attended, width), BF16),
        ),
        in_specs=[SMEM] + [VMEM] * 5,
        out_specs=(VMEM, HBM, VMEM, VMEM, VMEM),
        scratch_shapes=[pltpu.VMEM(pair_shape, kind) for kind in (F32, F32, F32, BF16)]
        + [
            pltpu.VMEM(queries.shape, BF16),
            pltpu.SemaphoreType.DMA((heads // 2,)),
        ],
        compiler_params=params,
        name="attend",
    )(me, queries, grad_out, order, live, got.reshape(-1, width))
    back = exchange(terms.reshape(cores * spans, 2 * rows, width), order_of)
    grad_keys, grad_values, log_totals, grad_queries = pl.pallas_call(
        functools.partial(sum_kernel, starts),
        out_shape=(
            shape(keys.shape, BF16),
            shape(keys.shape, BF16),
            shape((heads, tokens), F32),
            shape(queries.shape, BF16),
        ),
        in_specs=[SMEM] + [VMEM] * 5 + [HBM],
        out_specs=(HBM,) * 4,
        scratch_shapes=[
            pltpu.VMEM(keys.shape, BF16),
            pltpu.VMEM(keys.shape, BF16),
            pltpu.VMEM(queries.shape, BF16),
            pltpu.SemaphoreType.DMA((heads // 2 + 3,)),
        ],
        input_output_aliases={6: 3},
        compiler_params=params,
        name="sum_blocks",
    )(me, pick, back.reshape(-1, width), gs, k, logs, grad_queries)
    return grad_queries, log_totals, grad_keys, grad_values


def solution(mesh):
    in_specs = (
        P("seq", "vis"),
        P("seq", "vis", None),
        P("seq", "vis", None),
        P("seq", "vis"),
        P(),
        P(),
    )
    out_specs = (P("seq", "vis"), P("vis", "seq"), P("seq", "vis", None), P("seq", "vis", None))
    return jax.shard_map(local, mesh=mesh, in_specs=in_specs, out_specs=out_specs, check_vma=False)
```

```python
import functools
import math

import jax
import jax.numpy as jnp
import numpy as np
from jax import lax
from jax.experimental import pallas as pl
from jax.experimental.pallas import tpu as pltpu
from jax.sharding import PartitionSpec as P

HEAD_DIM = 128
GROUP = 8
BF16 = jnp.bfloat16
F32 = jnp.float32
LOG2E = math.log2(math.e)
VMEM = pl.BlockSpec(memory_space=pltpu.VMEM)
HBM = pl.BlockSpec(memory_space=pltpu.HBM)
SMEM = pl.BlockSpec(memory_space=pltpu.SMEM)
EXCHANGE_ORDER = {
    (16, 2): [18, 27, 28, 3, 6, 21, 13, 15, 22, 4, 12, 30, 7, 16, 23, 14, 20, 9, 17, 10, 29, 11, 0, 19, 26, 2, 24, 5, 1, 8, 31, 25],
}


def exchange_order(spans, cores):
    return EXCHANGE_ORDER.get((spans, cores)) or [span * cores + core for core in range(cores) for span in range(spans)]


def exchange(parts, order):
    return lax.all_to_all(
        parts, ("seq", "vis"), split_axis=0, concat_axis=0, tiled=True, axis_index_groups=[list(order)]
    )


def iota(shape, dim):
    return lax.broadcasted_iota(jnp.int32, shape, dim)


def dot(left, right, left_dim=1, right_dim=0):
    return lax.dot_general(
        left, right, (((left_dim,), (right_dim,)), ((), ())), preferred_element_type=F32
    )


def load_kernel(*refs):
    sems, half = refs[-1], len(refs) // 2
    copies = [pltpu.make_async_copy(src, dst, sems.at[i]) for i, (src, dst) in enumerate(zip(refs[:half], refs[half:-1]))]
    for copy in copies:
        copy.start()
    for copy in copies:
        copy.wait()


def choose_kernel(
    starts, me_ref, map_ref, count_ref, place_ref, keys_ref, values_ref, out_ref, pick_ref, order_ref, live_ref
):
    me = me_ref[0]
    per_owner, rows, _ = keys_ref.shape
    most, spans = map_ref.shape
    cores = len(starts)

    pick_rows, travelling = pick_ref.shape
    slot_rows = pick_rows // cores
    width = out_ref.shape[1]
    place_span, place_core = place_ref[0:1, :], place_ref[1:2, :]
    have, part = iota((pick_rows, 1), 0), iota((1, travelling), 1) % (2 * rows)
    have_slot = (have % (per_owner * rows) // rows + 1).astype(F32)
    same_part = have % slot_rows // (per_owner * rows) * rows + have % rows == part
    same_place = same_part & (have // slot_rows == place_core)

    block_rows = cores * rows
    keys = most * block_rows
    mine = iota((2 * keys, 1), 0)
    block = mine % keys // block_rows
    expand_blocks = (iota((2 * keys, most), 1) == block).astype(BF16)
    same_row = mine // keys * rows + mine % rows == part
    core = mine % block_rows // rows
    here = iota((1, spans), 1) == me
    live_block = iota(live_ref.shape, 0) // block_rows

    relative = map_ref[...] - me * per_owner
    asked = (relative >= 0) & (relative < per_owner) & (iota((most, spans), 0) < count_ref[...])
    slot = jnp.sum(jnp.where(asked, relative + 1, 0), axis=0, keepdims=True).astype(F32)
    lanes = 128
    slots = jnp.concatenate([slot, jnp.zeros((1, lanes - spans), F32)], axis=1)
    slots = jnp.broadcast_to(slots, (8, lanes))
    want = [
        jnp.take_along_axis(slots, jnp.broadcast_to(place_span[:, at : at + lanes], (8, lanes)), axis=1, mode="promise_in_bounds")[:1]
        for at in range(0, travelling, lanes)
    ]
    want = jnp.concatenate(want, axis=1)
    pick = ((want == have_slot) & same_place).astype(BF16)
    pick_ref[...] = pick
    stacked = [ref[slot].astype(F32) for ref in (keys_ref, values_ref) for slot in range(per_owner)]
    stacked = jnp.concatenate(stacked, axis=0).astype(BF16)
    stacked = jnp.concatenate([stacked[:, start : start + width] for start in starts], axis=0)
    out_ref[...] = dot(pick, stacked, 0, 0).astype(BF16)

    owners = jnp.sum(jnp.where(here, map_ref[...] // per_owner, 0), axis=1, keepdims=True)
    count = jnp.sum(jnp.where(here, count_ref[...], 0), axis=1, keepdims=True)
    lanes = jnp.broadcast_to(owners.astype(F32), (most, travelling)).astype(BF16)
    owner = dot(expand_blocks, lanes).astype(jnp.int32)
    order = same_row & (owner == place_span) & (core == place_core) & (block < count)
    order_ref[...] = order.astype(BF16)
    live_ref[...] = jnp.where(live_block < count, 0.0, -1e30)


def block_diagonal(part):
    zero = jnp.zeros_like(part)
    return jnp.concatenate([jnp.concatenate([part, zero], 1), jnp.concatenate([zero, part], 1)], 0)


def grad_queries_of(pair, gs_ref, k2, gq_ref, gq_hbm, sem):
    score_scale = 1.0 / math.sqrt(HEAD_DIM)
    at = slice(2 * pair * HEAD_DIM, 2 * (pair + 1) * HEAD_DIM)
    gq_ref[:, at] = (dot(gs_ref[pair], k2, 0, 0) * score_scale).astype(BF16)
    copy = pltpu.make_async_copy(gq_ref.at[:, at], gq_hbm.at[:, at], sem)
    copy.start()
    return copy


def attend_body(
    early, q_ref, g_ref, order_ref, live_ref, rows_ref, terms_ref, gq_hbm, log_ref, gs_ref, k_ref,
    scores_ref, gp_ref, probs_ref, low_ref, gq_ref, sems
):
    score_scale = 1.0 / math.sqrt(HEAD_DIM)
    keys, tokens = live_ref.shape
    kv_heads = rows_ref.shape[1] // HEAD_DIM
    pairs = gs_ref.shape[0]
    split, joined = (2, keys, tokens), (2 * keys, tokens)
    columns = [slice(2 * pair * HEAD_DIM, 2 * (pair + 1) * HEAD_DIM) for pair in range(pairs)]
    order, live = order_ref[...], live_ref[...]
    fetched = dot(order, rows_ref[...]).astype(BF16)
    k_ref[...] = fetched[:keys]
    heads = [fetched[:, kv * HEAD_DIM : (kv + 1) * HEAD_DIM] for kv in range(kv_heads)]
    k2 = [block_diagonal(head[:keys]) for head in heads for _ in range(pairs // kv_heads)]
    v2 = [block_diagonal(head[keys:]) for head in heads for _ in range(pairs // kv_heads)]

    copies = []
    gk, gv = [0.0] * kv_heads, [0.0] * kv_heads

    def score(pair):
        scores_ref[pair] = dot(k2[pair], q_ref[:, columns[pair]], 1, 1)

    def soften(pair):
        scores = scores_ref[pair].reshape(split) * (score_scale * LOG2E) + live
        row_max = jnp.max(scores, axis=1, keepdims=True)
        weights = jnp.exp2(scores - row_max)
        totals = jnp.sum(weights, axis=1, keepdims=True)
        probs = weights * (1.0 / totals)
        log_ref[2 * pair : 2 * pair + 2, :] = ((row_max + jnp.log2(totals)) * (1.0 / LOG2E)).reshape(2, tokens)
        probs_ref[pair] = probs.reshape(joined)
        low_ref[pair] = probs.astype(BF16).reshape(joined)

    def against_values(pair):
        gp_ref[pair] = dot(v2[pair], g_ref[:, columns[pair]], 1, 1)

    def grad_score(pair):
        grad_probs = gp_ref[pair].reshape(split)
        delta = jnp.sum(low_ref[pair].reshape(split).astype(F32) * grad_probs, axis=1, keepdims=True)
        gs_ref[pair] = (probs_ref[pair].reshape(split) * (grad_probs - delta)).astype(BF16).reshape(joined)

    def add_values(pair):
        gv[pair * kv_heads // pairs] += dot(low_ref[pair], g_ref[:, columns[pair]])

    def add_keys(pair):
        gk[pair * kv_heads // pairs] += dot(gs_ref[pair], q_ref[:, columns[pair]])

    def add_queries(pair):
        if early:
            copies.append(grad_queries_of(pair, gs_ref, k2[pair], gq_ref, gq_hbm, sems.at[pair]))

    for pair in range(pairs):
        score(pair)
        against_values(pair)
    for pair in range(pairs):
        soften(pair)
        if not early:
            add_values(pair)
    for pair in range(pairs):
        grad_score(pair)
    for pair in range(pairs):
        add_queries(pair)
    for pair in range(pairs):
        add_keys(pair)
        if early:
            add_values(pair)
    gk = [(part[:keys, :HEAD_DIM] + part[keys:, HEAD_DIM:]) * score_scale for part in gk]
    gv = [part[:keys, :HEAD_DIM] + part[keys:, HEAD_DIM:] for part in gv]
    terms = jnp.concatenate([jnp.concatenate(gk, 1), jnp.concatenate(gv, 1)], 0).astype(BF16)
    terms_ref[...] = dot(order, terms, 0, 0).astype(BF16)
    for copy in copies:
        copy.wait()


def attend_kernel(me_ref, *refs):
    pl.when(me_ref[0] == 0)(lambda: attend_body(True, *refs))
    pl.when(me_ref[0] != 0)(lambda: attend_body(False, *refs))


def sum_kernel(
    starts, me_ref, pick_ref, terms_ref, gs_ref, k_ref, log_ref, _, keys_hbm, values_hbm, log_hbm, gq_hbm,
    keys_ref, values_ref, gq_ref, sems
):
    per_owner, rows, _ = keys_ref.shape
    width = terms_ref.shape[1]
    totals = dot(pick_ref[...], terms_ref[...])
    slot_rows = 2 * per_owner * rows
    done = {}
    for core, start in enumerate(starts):
        part = totals[core * slot_rows : (core + 1) * slot_rows]
        done[start] = done[start] + part if start in done else part
    for start, total in done.items():
        for slot in range(per_owner):
            for place, ref in ((slot, keys_ref), (per_owner + slot, values_ref)):
                ref[slot, :, start : start + width] = total[place * rows : (place + 1) * rows].astype(BF16)
    pairs = gs_ref.shape[0]
    copies = [
        pltpu.make_async_copy(keys_ref, keys_hbm, sems.at[pairs]),
        pltpu.make_async_copy(values_ref, values_hbm, sems.at[pairs + 1]),
        pltpu.make_async_copy(log_ref, log_hbm, sems.at[pairs + 2]),
    ]
    for copy in copies:
        copy.start()

    @pl.when(me_ref[0] != 0)
    def _():
        kv_heads = k_ref.shape[1] // HEAD_DIM
        k2 = [block_diagonal(k_ref[:, kv * HEAD_DIM : (kv + 1) * HEAD_DIM]) for kv in range(kv_heads)]
        late = [
            grad_queries_of(pair, gs_ref, k2[pair * kv_heads // pairs], gq_ref, gq_hbm, sems.at[pair])
            for pair in range(pairs)
        ]
        for copy in late:
            copy.wait()

    for copy in copies:
        copy.wait()


def local(queries, keys, values, grad_out, block_map, block_count):
    spans, cores = lax.axis_size("seq"), lax.axis_size("vis")
    me = lax.axis_index("seq").astype(jnp.int32).reshape(1)
    per_owner, rows, _ = keys.shape
    tokens = queries.shape[0]
    heads = queries.shape[1] // HEAD_DIM
    most = block_map.shape[1]
    width = max(heads // GROUP, 1) * HEAD_DIM
    starts = tuple(core * heads // GROUP * HEAD_DIM for core in range(cores))
    attended = most * cores * rows
    travelling = cores * spans * 2 * rows
    order_of = exchange_order(spans, cores)
    places = jnp.asarray(np.repeat(np.divmod(np.array(order_of, np.int32), cores), 2 * rows, axis=1))
    shape = jax.ShapeDtypeStruct
    params = pltpu.CompilerParams(vmem_limit_bytes=24 * 1024 * 1024)
    stay = functools.partial(pltpu.with_memory_space_constraint, memory_space=pltpu.HBM)

    inputs = (block_map.T, block_count.reshape(1, spans), places)
    inputs = pl.pallas_call(
        load_kernel,
        out_shape=tuple(shape(part.shape, part.dtype) for part in inputs),
        in_specs=[HBM] * 3,
        out_specs=(VMEM,) * 3,
        scratch_shapes=[pltpu.SemaphoreType.DMA((3,))],
        compiler_params=params,
        cost_estimate=pl.CostEstimate(flops=10**9, bytes_accessed=10**6, transcendentals=0),
        name="load_blocks",
    )(*map(stay, inputs))
    sent, pick, order, live = pl.pallas_call(
        functools.partial(choose_kernel, starts),
        out_shape=(
            shape((travelling, width), BF16),
            shape((cores * 2 * per_owner * rows, travelling), BF16),
            shape((2 * attended, travelling), BF16),
            shape((attended, tokens), F32),
        ),
        in_specs=[SMEM] + [VMEM] * 5,
        out_specs=(VMEM,) * 4,
        compiler_params=params,
        cost_estimate=pl.CostEstimate(flops=10**10, bytes_accessed=10**6, transcendentals=0),
        name="choose_blocks",
    )(me, *inputs, keys, values)
    got = exchange(sent.reshape(cores * spans, 2 * rows, width), order_of)
    pair_shape = (heads // 2, 2 * attended, tokens)
    terms, grad_queries, logs, gs, k = pl.pallas_call(
        attend_kernel,
        out_shape=(
            shape((travelling, width), BF16),
            shape(queries.shape, BF16),
            shape((heads, tokens), F32),
            shape(pair_shape, BF16),
            shape((attended, width), BF16),
        ),
        in_specs=[SMEM] + [VMEM] * 5,
        out_specs=(VMEM, HBM, VMEM, VMEM, VMEM),
        scratch_shapes=[pltpu.VMEM(pair_shape, kind) for kind in (F32, F32, F32, BF16)]
        + [
            pltpu.VMEM(queries.shape, BF16),
            pltpu.SemaphoreType.DMA((heads // 2,)),
        ],
        compiler_params=params,
        name="attend",
    )(me, queries, grad_out, order, live, got.reshape(-1, width))
    back = exchange(terms.reshape(cores * spans, 2 * rows, width), order_of)
    grad_keys, grad_values, log_totals, grad_queries = pl.pallas_call(
        functools.partial(sum_kernel, starts),
        out_shape=(
            shape(keys.shape, BF16),
            shape(keys.shape, BF16),
            shape((heads, tokens), F32),
            shape(queries.shape, BF16),
        ),
        in_specs=[SMEM] + [VMEM] * 5 + [HBM],
        out_specs=(HBM,) * 4,
        scratch_shapes=[
            pltpu.VMEM(keys.shape, BF16),
            pltpu.VMEM(keys.shape, BF16),
            pltpu.VMEM(queries.shape, BF16),
            pltpu.SemaphoreType.DMA((heads // 2 + 3,)),
        ],
        input_output_aliases={6: 3},
        compiler_params=params,
        name="sum_blocks",
    )(me, pick, back.reshape(-1, width), gs, k, logs, grad_queries)
    return grad_queries, log_totals, grad_keys, grad_values


def solution(mesh):
    in_specs = (
        P("seq", "vis"),
        P("seq", "vis", None),
        P("seq", "vis", None),
        P("seq", "vis"),
        P(),
        P(),
    )
    out_specs = (P("seq", "vis"), P("vis", "seq"), P("seq", "vis", None), P("seq", "vis", None))
    return jax.shard_map(local, mesh=mesh, in_specs=in_specs, out_specs=out_specs, check_vma=False)
```

```python
import functools
import math

import jax
import jax.numpy as jnp
import numpy as np
from jax import lax
from jax.experimental import pallas as pl
from jax.experimental.pallas import tpu as pltpu
from jax.sharding import PartitionSpec as P

HEAD_DIM = 128
GROUP = 8
BF16 = jnp.bfloat16
F32 = jnp.float32
LOG2E = math.log2(math.e)
VMEM = pl.BlockSpec(memory_space=pltpu.VMEM)
HBM = pl.BlockSpec(memory_space=pltpu.HBM)
SMEM = pl.BlockSpec(memory_space=pltpu.SMEM)
EXCHANGE_ORDER = {
    (16, 2): [21, 27, 28, 3, 29, 18, 13, 15, 22, 20, 12, 30, 7, 16, 23, 14, 4, 1, 17, 10, 6, 11, 0, 19, 26, 2, 24, 5, 9, 8, 31, 25],
}


def exchange_order(spans, cores):
    return EXCHANGE_ORDER.get((spans, cores)) or [span * cores + core for core in range(cores) for span in range(spans)]


def exchange(parts, order):
    return lax.all_to_all(
        parts, ("seq", "vis"), split_axis=0, concat_axis=0, tiled=True, axis_index_groups=[list(order)]
    )


def iota(shape, dim):
    return lax.broadcasted_iota(jnp.int32, shape, dim)


def dot(left, right, left_dim=1, right_dim=0):
    return lax.dot_general(
        left, right, (((left_dim,), (right_dim,)), ((), ())), preferred_element_type=F32
    )


def load_kernel(*refs):
    sems, half = refs[-1], len(refs) // 2
    copies = [pltpu.make_async_copy(src, dst, sems.at[i]) for i, (src, dst) in enumerate(zip(refs[:half], refs[half:-1]))]
    for copy in copies:
        copy.start()
    for copy in copies:
        copy.wait()


def choose_kernel(
    starts, me_ref, map_ref, count_ref, place_ref, keys_ref, values_ref, out_ref, pick_ref, order_ref, live_ref
):
    me = me_ref[0]
    per_owner, rows, _ = keys_ref.shape
    most, spans = map_ref.shape
    cores = len(starts)

    pick_rows, travelling = pick_ref.shape
    slot_rows = pick_rows // cores
    width = out_ref.shape[1]
    place_span, place_core = place_ref[0:1, :], place_ref[1:2, :]
    have, part = iota((pick_rows, 1), 0), iota((1, travelling), 1) % (2 * rows)
    have_slot = (have % (per_owner * rows) // rows + 1).astype(F32)
    same_part = have % slot_rows // (per_owner * rows) * rows + have % rows == part
    same_place = same_part & (have // slot_rows == place_core)

    block_rows = cores * rows
    keys = most * block_rows
    mine = iota((2 * keys, 1), 0)
    block = mine % keys // block_rows
    expand_blocks = (iota((2 * keys, most), 1) == block).astype(BF16)
    same_row = mine // keys * rows + mine % rows == part
    core = mine % block_rows // rows
    here = iota((1, spans), 1) == me
    live_block = iota(live_ref.shape, 0) // block_rows

    relative = map_ref[...] - me * per_owner
    asked = (relative >= 0) & (relative < per_owner) & (iota((most, spans), 0) < count_ref[...])
    slot = jnp.sum(jnp.where(asked, relative + 1, 0), axis=0, keepdims=True).astype(F32)
    lanes = 128
    slots = jnp.concatenate([slot, jnp.zeros((1, lanes - spans), F32)], axis=1)
    slots = jnp.broadcast_to(slots, (8, lanes))
    want = [
        jnp.take_along_axis(slots, jnp.broadcast_to(place_span[:, at : at + lanes], (8, lanes)), axis=1, mode="promise_in_bounds")[:1]
        for at in range(0, travelling, lanes)
    ]
    want = jnp.concatenate(want, axis=1)
    pick = ((want == have_slot) & same_place).astype(BF16)
    pick_ref[...] = pick
    stacked = [ref[slot].astype(F32) for ref in (keys_ref, values_ref) for slot in range(per_owner)]
    stacked = jnp.concatenate(stacked, axis=0).astype(BF16)
    stacked = jnp.concatenate([stacked[:, start : start + width] for start in starts], axis=0)
    out_ref[...] = dot(pick, stacked, 0, 0).astype(BF16)

    owners = jnp.sum(jnp.where(here, map_ref[...] // per_owner, 0), axis=1, keepdims=True)
    count = jnp.sum(jnp.where(here, count_ref[...], 0), axis=1, keepdims=True)
    lanes = jnp.broadcast_to(owners.astype(F32), (most, travelling)).astype(BF16)
    owner = dot(expand_blocks, lanes).astype(jnp.int32)
    order = same_row & (owner == place_span) & (core == place_core) & (block < count)
    order_ref[...] = order.astype(BF16)
    live_ref[...] = jnp.where(live_block < count, 0.0, -1e30)


def block_diagonal(part):
    zero = jnp.zeros_like(part)
    return jnp.concatenate([jnp.concatenate([part, zero], 1), jnp.concatenate([zero, part], 1)], 0)


def grad_queries_of(pair, gs_ref, k2, gq_ref, gq_hbm, sem):
    score_scale = 1.0 / math.sqrt(HEAD_DIM)
    at = slice(2 * pair * HEAD_DIM, 2 * (pair + 1) * HEAD_DIM)
    gq_ref[:, at] = (dot(gs_ref[pair], k2, 0, 0) * score_scale).astype(BF16)
    copy = pltpu.make_async_copy(gq_ref.at[:, at], gq_hbm.at[:, at], sem)
    copy.start()
    return copy


def attend_body(
    early, q_ref, g_ref, order_ref, live_ref, rows_ref, terms_ref, gq_hbm, log_ref, gs_ref, k_ref,
    scores_ref, gp_ref, probs_ref, low_ref, gq_ref, sems
):
    score_scale = 1.0 / math.sqrt(HEAD_DIM)
    keys, tokens = live_ref.shape
    kv_heads = rows_ref.shape[1] // HEAD_DIM
    pairs = gs_ref.shape[0]
    split, joined = (2, keys, tokens), (2 * keys, tokens)
    columns = [slice(2 * pair * HEAD_DIM, 2 * (pair + 1) * HEAD_DIM) for pair in range(pairs)]
    order, live = order_ref[...], live_ref[...]
    fetched = dot(order, rows_ref[...]).astype(BF16)
    k_ref[...] = fetched[:keys]
    heads = [fetched[:, kv * HEAD_DIM : (kv + 1) * HEAD_DIM] for kv in range(kv_heads)]
    k2 = [block_diagonal(head[:keys]) for head in heads for _ in range(pairs // kv_heads)]
    v2 = [block_diagonal(head[keys:]) for head in heads for _ in range(pairs // kv_heads)]

    copies = []
    gk, gv = [0.0] * kv_heads, [0.0] * kv_heads

    def score(pair):
        scores_ref[pair] = dot(k2[pair], q_ref[:, columns[pair]], 1, 1)

    def soften(pair):
        scores = scores_ref[pair].reshape(split) * (score_scale * LOG2E) + live
        row_max = jnp.max(scores, axis=1, keepdims=True)
        weights = jnp.exp2(scores - row_max)
        totals = jnp.sum(weights, axis=1, keepdims=True)
        probs = weights * (1.0 / totals)
        log_ref[2 * pair : 2 * pair + 2, :] = ((row_max + jnp.log2(totals)) * (1.0 / LOG2E)).reshape(2, tokens)
        probs_ref[pair] = probs.reshape(joined)
        low_ref[pair] = probs.astype(BF16).reshape(joined)

    def against_values(pair):
        gp_ref[pair] = dot(v2[pair], g_ref[:, columns[pair]], 1, 1)

    def grad_score(pair):
        grad_probs = gp_ref[pair].reshape(split)
        delta = jnp.sum(low_ref[pair].reshape(split).astype(F32) * grad_probs, axis=1, keepdims=True)
        gs_ref[pair] = (probs_ref[pair].reshape(split) * (grad_probs - delta)).astype(BF16).reshape(joined)

    def add_values(pair):
        gv[pair * kv_heads // pairs] += dot(low_ref[pair], g_ref[:, columns[pair]])

    def add_keys(pair):
        gk[pair * kv_heads // pairs] += dot(gs_ref[pair], q_ref[:, columns[pair]])

    def add_queries(pair):
        if early:
            copies.append(grad_queries_of(pair, gs_ref, k2[pair], gq_ref, gq_hbm, sems.at[pair]))

    for pair in range(pairs):
        score(pair)
        against_values(pair)
    for pair in range(pairs):
        soften(pair)
        if not early:
            add_values(pair)
    for pair in range(pairs):
        grad_score(pair)
    for pair in range(pairs):
        add_queries(pair)
    for pair in range(pairs):
        add_keys(pair)
        if early:
            add_values(pair)
    gk = [(part[:keys, :HEAD_DIM] + part[keys:, HEAD_DIM:]) * score_scale for part in gk]
    gv = [part[:keys, :HEAD_DIM] + part[keys:, HEAD_DIM:] for part in gv]
    terms = jnp.concatenate([jnp.concatenate(gk, 1), jnp.concatenate(gv, 1)], 0).astype(BF16)
    terms_ref[...] = dot(order, terms, 0, 0).astype(BF16)
    for copy in copies:
        copy.wait()


def attend_kernel(me_ref, *refs):
    pl.when(me_ref[0] == 0)(lambda: attend_body(True, *refs))
    pl.when(me_ref[0] != 0)(lambda: attend_body(False, *refs))


def sum_kernel(
    starts, me_ref, pick_ref, terms_ref, gs_ref, k_ref, log_ref, _, keys_hbm, values_hbm, log_hbm, gq_hbm,
    keys_ref, values_ref, gq_ref, sems
):
    per_owner, rows, _ = keys_ref.shape
    width = terms_ref.shape[1]
    totals = dot(pick_ref[...], terms_ref[...])
    slot_rows = 2 * per_owner * rows
    done = {}
    for core, start in enumerate(starts):
        part = totals[core * slot_rows : (core + 1) * slot_rows]
        done[start] = done[start] + part if start in done else part
    for start, total in done.items():
        for slot in range(per_owner):
            for place, ref in ((slot, keys_ref), (per_owner + slot, values_ref)):
                ref[slot, :, start : start + width] = total[place * rows : (place + 1) * rows].astype(BF16)
    pairs = gs_ref.shape[0]
    copies = [
        pltpu.make_async_copy(keys_ref, keys_hbm, sems.at[pairs]),
        pltpu.make_async_copy(values_ref, values_hbm, sems.at[pairs + 1]),
        pltpu.make_async_copy(log_ref, log_hbm, sems.at[pairs + 2]),
    ]
    for copy in copies:
        copy.start()

    @pl.when(me_ref[0] != 0)
    def _():
        kv_heads = k_ref.shape[1] // HEAD_DIM
        k2 = [block_diagonal(k_ref[:, kv * HEAD_DIM : (kv + 1) * HEAD_DIM]) for kv in range(kv_heads)]
        late = [
            grad_queries_of(pair, gs_ref, k2[pair * kv_heads // pairs], gq_ref, gq_hbm, sems.at[pair])
            for pair in range(pairs)
        ]
        for copy in late:
            copy.wait()

    for copy in copies:
        copy.wait()


def local(queries, keys, values, grad_out, block_map, block_count):
    spans, cores = lax.axis_size("seq"), lax.axis_size("vis")
    me = lax.axis_index("seq").astype(jnp.int32).reshape(1)
    per_owner, rows, _ = keys.shape
    tokens = queries.shape[0]
    heads = queries.shape[1] // HEAD_DIM
    most = block_map.shape[1]
    width = max(heads // GROUP, 1) * HEAD_DIM
    starts = tuple(core * heads // GROUP * HEAD_DIM for core in range(cores))
    attended = most * cores * rows
    travelling = cores * spans * 2 * rows
    order_of = exchange_order(spans, cores)
    places = jnp.asarray(np.repeat(np.divmod(np.array(order_of, np.int32), cores), 2 * rows, axis=1))
    shape = jax.ShapeDtypeStruct
    params = pltpu.CompilerParams(vmem_limit_bytes=24 * 1024 * 1024)
    stay = functools.partial(pltpu.with_memory_space_constraint, memory_space=pltpu.HBM)

    inputs = (block_map.T, block_count.reshape(1, spans), places)
    inputs = pl.pallas_call(
        load_kernel,
        out_shape=tuple(shape(part.shape, part.dtype) for part in inputs),
        in_specs=[HBM] * 3,
        out_specs=(VMEM,) * 3,
        scratch_shapes=[pltpu.SemaphoreType.DMA((3,))],
        compiler_params=params,
        cost_estimate=pl.CostEstimate(flops=10**9, bytes_accessed=10**6, transcendentals=0),
        name="load_blocks",
    )(*map(stay, inputs))
    sent, pick, order, live = pl.pallas_call(
        functools.partial(choose_kernel, starts),
        out_shape=(
            shape((travelling, width), BF16),
            shape((cores * 2 * per_owner * rows, travelling), BF16),
            shape((2 * attended, travelling), BF16),
            shape((attended, tokens), F32),
        ),
        in_specs=[SMEM] + [VMEM] * 5,
        out_specs=(VMEM,) * 4,
        compiler_params=params,
        cost_estimate=pl.CostEstimate(flops=10**10, bytes_accessed=10**6, transcendentals=0),
        name="choose_blocks",
    )(me, *inputs, keys, values)
    got = exchange(sent.reshape(cores * spans, 2 * rows, width), order_of)
    pair_shape = (heads // 2, 2 * attended, tokens)
    terms, grad_queries, logs, gs, k = pl.pallas_call(
        attend_kernel,
        out_shape=(
            shape((travelling, width), BF16),
            shape(queries.shape, BF16),
            shape((heads, tokens), F32),
            shape(pair_shape, BF16),
            shape((attended, width), BF16),
        ),
        in_specs=[SMEM] + [VMEM] * 5,
        out_specs=(VMEM, HBM, VMEM, VMEM, VMEM),
        scratch_shapes=[pltpu.VMEM(pair_shape, kind) for kind in (F32, F32, F32, BF16)]
        + [
            pltpu.VMEM(queries.shape, BF16),
            pltpu.SemaphoreType.DMA((heads // 2,)),
        ],
        compiler_params=params,
        name="attend",
    )(me, queries, grad_out, order, live, got.reshape(-1, width))
    back = exchange(terms.reshape(cores * spans, 2 * rows, width), order_of)
    grad_keys, grad_values, log_totals, grad_queries = pl.pallas_call(
        functools.partial(sum_kernel, starts),
        out_shape=(
            shape(keys.shape, BF16),
            shape(keys.shape, BF16),
            shape((heads, tokens), F32),
            shape(queries.shape, BF16),
        ),
        in_specs=[SMEM] + [VMEM] * 5 + [HBM],
        out_specs=(HBM,) * 4,
        scratch_shapes=[
            pltpu.VMEM(keys.shape, BF16),
            pltpu.VMEM(keys.shape, BF16),
            pltpu.VMEM(queries.shape, BF16),
            pltpu.SemaphoreType.DMA((heads // 2 + 3,)),
        ],
        input_output_aliases={6: 3},
        compiler_params=params,
        name="sum_blocks",
    )(me, pick, back.reshape(-1, width), gs, k, logs, grad_queries)
    return grad_queries, log_totals, grad_keys, grad_values


def solution(mesh):
    in_specs = (
        P("seq", "vis"),
        P("seq", "vis", None),
        P("seq", "vis", None),
        P("seq", "vis"),
        P(),
        P(),
    )
    out_specs = (P("seq", "vis"), P("vis", "seq"), P("seq", "vis", None), P("seq", "vis", None))
    return jax.shard_map(local, mesh=mesh, in_specs=in_specs, out_specs=out_specs, check_vma=False)
```
